512 devices in a mesh: wide: 64 (over z, x), narrow: 8 (over y, core).
Axes of the slice: x: 4, y: 4, z: 16, core: 2. Of those that a mesh axis runs over, the one named last changes fastest.
Arguments:
- row_embed: float32 [12288, 512], P(('wide', 'narrow')), may hold values from -10 to 10
- col_embed: float32 [12288, 512], P(('wide', 'narrow')), may hold values from -10 to 10
- logit_scale: float32 [], replicated, may hold values from 1.5 to 3
- targets: int32 [12288], P(('wide', 'narrow')), may hold values from 0 to 12287, each once
Outputs:
- row_grads: float32 [12288, 512], P(('wide', 'narrow'))
- col_grads: float32 [12288, 512], P(('wide', 'narrow'))
The draws below stay inside these ranges and needn't reach their ends.
All inputs are finite; a program needn't handle non-finite values.
Results may differ from the reference program's by a relative error of at most 0.0005.
Values sent between devices are 32-bit elements; how exact they have to be, the bound alone decides.
No kernel may reach another device: no remote copies, remote signals or barrier semaphores. Data moves between devices by JAX's collectives and lax.ppermute only.
A program may use at most 64 MiB of HBM per device.

```python
import math
import jax
import jax.numpy as jnp
from jax import lax

D = 512
N = 12288


def row_scales(key, number_rows):
    uniform_part = jax.random.uniform(key, (number_rows,), jnp.float32, 0.0, 1.0)
    rising = 1.0 + 2.0 * jnp.arange(number_rows, dtype=jnp.float32) / number_rows
    return jnp.exp(uniform_part * math.log(10.0)) * rising / 3.0


def draw_row_embed(key, part):
    key = jax.random.fold_in(key, 11)
    key_scale, key_jitter = jax.random.split(key)
    scales = row_scales(key_scale, N)
    jitter = jax.random.truncated_normal(key_jitter, -5.0, 5.0, (N, D), jnp.float32)
    values = scales[:, None] * jitter / math.sqrt(D)
    return values


def draw_col_embed(key, part):
    key = jax.random.fold_in(key, 23)
    key_scale, key_jitter = jax.random.split(key, 2)
    scales = row_scales(key_scale, N)
    jitter = jax.random.truncated_normal(key_jitter, -5.0, 5.0, (N, D), jnp.float32)
    values = scales[:, None] * jitter / math.sqrt(D)
    return values


def setup_inputs(seed: int = 0) -> dict:
    key_list = jax.random.split(jax.random.key(seed), 5)
    return {
        "row_embed": draw_row_embed(jax.random.fold_in(key_list[4], 71), 0),
        "col_embed": draw_col_embed(jax.random.fold_in(key_list[4], 71), 0),
        "logit_scale": jnp.clip(jnp.exp(jax.random.uniform(key_list[2], (), jnp.float32, math.log(1.5), math.log(3.0))), 1.5, 3.0),
        "targets": jax.random.permutation(key_list[3], N).astype(jnp.int32),
    }


def reference(row_embed, col_embed, logit_scale, targets):
    total_rows = row_embed.shape[0]
    block_size = math.gcd(total_rows, 512)
    block_count = total_rows // block_size
    row_blocks = row_embed.reshape(block_count, block_size, D)
    target_blocks = targets.reshape(block_count, block_size)
    highest = lax.Precision.HIGHEST

    def statistics(running, blocks):
        col_top, col_total = running
        scores = logit_scale * jnp.dot(blocks, col_embed.T, precision=highest, preferred_element_type=jnp.float32)
        row_top = jnp.max(scores, axis=1)
        row_lse = row_top + jnp.log(jnp.sum(jnp.exp(scores - row_top[:, None]), axis=1))
        highest_col = jnp.maximum(col_top, jnp.max(scores, axis=0))
        col_total = col_total * jnp.exp(col_top - highest_col) + jnp.sum(jnp.exp(scores - highest_col[None, :]), axis=0)
        return (highest_col, col_total), row_lse

    start_running = (jnp.full((total_rows,), -1e30, jnp.float32), jnp.zeros((total_rows,), jnp.float32))
    (col_top, col_total), row_lse = lax.scan(statistics, start_running, row_blocks)
    col_lse = col_top + jnp.log(col_total)
    column_ids = jnp.arange(total_rows, dtype=jnp.int32)

    def gradients(grad_cols, blocks):
        block_rows, block_targets, block_lse = blocks
        scores = logit_scale * jnp.dot(block_rows, col_embed.T, precision=highest, preferred_element_type=jnp.float32)
        positive = (block_targets[:, None] == column_ids[None, :]).astype(jnp.float32)
        weights = 0.5 * jnp.exp(scores - block_lse[:, None]) + 0.5 * jnp.exp(scores - col_lse[None, :]) - positive
        grad_rows = logit_scale * jnp.dot(weights, col_embed, precision=highest, preferred_element_type=jnp.float32)
        grad_cols = grad_cols + logit_scale * jnp.dot(weights.T, block_rows, precision=highest, preferred_element_type=jnp.float32)
        return grad_cols, grad_rows

    grad_cols, grad_rows = lax.scan(gradients, jnp.zeros((total_rows, D), jnp.float32), (row_blocks, target_blocks, row_lse))
    return grad_rows.reshape(total_rows, D), grad_cols
```

```python
import jax
import jax.numpy as jnp
from jax import lax
from jax.sharding import Mesh, PartitionSpec as P

ALL = ("z", "x", "y", "core")
Z, XY, CORE = 16, 16, 2
SWAP = [(0, 1), (1, 0)]


def to_all(block, axes, count):
    sent = jnp.broadcast_to(block[None], (count,) + block.shape)
    return lax.all_to_all(sent, axes, 0, 0, tiled=True)


def combine(tops, totals):
    top = jnp.max(tops, axis=0)
    return top, jnp.sum(totals * jnp.exp(tops - top[None]), axis=0)


def core_pair(block, core):
    other = lax.ppermute(block, "core", SWAP)
    return jnp.where(core == 0, jnp.stack([block, other]), jnp.stack([other, block]))


def local(row_embed, col_embed, logit_scale, targets):
    own, width = row_embed.shape
    core = lax.axis_index("core")
    plane = lax.axis_index("z")
    cols = to_all(col_embed, ("x", "y"), XY).reshape(XY * own, width)
    rows = to_all(row_embed, "z", Z).reshape(Z * own, width)
    cols = core_pair(cols, core).reshape(CORE * XY * own, width)
    row_count, col_count = rows.shape[0], cols.shape[0]

    scores = logit_scale * lax.dot_general(
        rows, cols, (((1,), (1,)), ((), ())),
        precision=lax.Precision.HIGHEST, preferred_element_type=jnp.float32,
    )
    row_top = jnp.max(scores, axis=1)
    row_total = jnp.sum(jnp.exp(scores - row_top[:, None]), axis=1)
    col_top = jnp.max(scores, axis=0)
    col_total = jnp.sum(jnp.exp(scores - col_top[None, :]), axis=0)

    row_message = jnp.concatenate(
        [row_top, row_total, targets.astype(jnp.float32), jnp.zeros((1024 - 2 * row_count - own,), jnp.float32)]
    ).reshape(8, 128)
    row_stats = to_all(row_message, "z", Z).reshape(Z, 1024)
    row_top, row_total = combine(row_stats[:, :row_count], row_stats[:, row_count:2 * row_count])
    row_targets = row_stats[:, 2 * row_count:2 * row_count + own].reshape(row_count).astype(jnp.int32)

    col_message = jnp.concatenate([col_top, col_total]).reshape(12, 128)
    pair = core_pair(col_message, core).reshape(CORE, 2, col_count)
    col_message = jnp.concatenate(combine(pair[:, 0], pair[:, 1])).reshape(12, 128)
    col_stats = to_all(col_message, ("x", "y"), XY).reshape(XY, 2, col_count)
    col_top, col_total = combine(col_stats[:, 0], col_stats[:, 1])

    place = jnp.arange(col_count, dtype=jnp.int32)
    place_core, place_chip, place_own = place // (XY * own), place // own % XY, place % own
    column_ids = ((plane * XY + place_chip) * CORE + place_core) * own + place_own
    weights = (
        jnp.exp(scores - row_top[:, None]) * (0.5 / row_total)[:, None]
        + jnp.exp(scores - col_top[None, :]) * (0.5 / col_total)[None, :]
        - (row_targets[:, None] == column_ids[None, :]).astype(jnp.float32)
    )
    grad_rows = lax.dot_general(
        weights, cols, (((1,), (0,)), ((), ())),
        precision=lax.Precision.HIGH, preferred_element_type=jnp.float32,
    )
    grad_cols = lax.dot_general(
        weights, rows, (((0,), (0,)), ((), ())),
        precision=lax.Precision.HIGH, preferred_element_type=jnp.float32,
    ).reshape(CORE, XY * own, width)
    mine = lax.dynamic_index_in_dim(grad_cols, core, 0, keepdims=False)
    theirs = lax.dynamic_index_in_dim(grad_cols, 1 - core, 0, keepdims=False)
    grad_cols = mine + lax.ppermute(theirs, "core", SWAP)
    row_parts = lax.all_to_all(grad_rows.reshape(Z, own, width), "z", 0, 0, tiled=True)
    col_parts = lax.all_to_all(grad_cols.reshape(XY, own, width), ("x", "y"), 0, 0, tiled=True)
    return logit_scale * jnp.sum(row_parts, axis=0), logit_scale * jnp.sum(col_parts, axis=0)


def solution(mesh):
    grid = Mesh(mesh.devices.reshape(Z, 4, 4, CORE), ALL)
    placed = P(ALL, None)
    return jax.shard_map(
        local, mesh=grid, in_specs=(placed, placed, P(), P(ALL)), out_specs=(placed, placed), check_vma=False
    )
```

```python
import jax
import jax.numpy as jnp
from jax import lax
from jax.sharding import Mesh, PartitionSpec as P

ALL = ("z", "x", "y", "core")
Z, SIDE, CORE = 16, 4, 2


def shift(block, axis, count, by):
    return lax.ppermute(block, axis, [(i, (i + by) % count) for i in range(count)])


def around(block, axis, count):
    return jnp.stack([block] + [shift(block, axis, count, by) for by in range(1, count)])


def home(parts, axis, count):
    total = parts[0]
    for by in range(1, count):
        total = total + shift(parts[by], axis, count, -by)
    return total


def combine(tops, totals):
    top = jnp.max(tops, axis=0)
    return top, jnp.sum(totals * jnp.exp(tops - top[None]), axis=0)


def local(row_embed, col_embed, logit_scale, targets):
    own, width = row_embed.shape
    plane, across, along, core = (lax.axis_index(a) for a in ALL)
    rows = lax.all_to_all(
        jnp.broadcast_to(row_embed[None], (Z, own, width)), "z", 0, 0, tiled=True
    ).reshape(Z * own, width)
    cols = around(col_embed, "x", SIDE)
    cols = around(cols, "y", SIDE)
    cols = around(cols, "core", CORE).reshape(CORE * SIDE * SIDE * own, width)
    row_count, col_count = rows.shape[0], cols.shape[0]

    scores = logit_scale * lax.dot_general(
        rows, cols, (((1,), (1,)), ((), ())),
        precision=lax.Precision.HIGHEST, preferred_element_type=jnp.float32,
    )
    row_top = jnp.max(scores, axis=1)
    row_total = jnp.sum(jnp.exp(scores - row_top[:, None]), axis=1)
    col_top = jnp.max(scores, axis=0)
    col_total = jnp.sum(jnp.exp(scores - col_top[None, :]), axis=0)

    row_message = jnp.concatenate(
        [row_top, row_total, targets.astype(jnp.float32), jnp.zeros((1024 - 2 * row_count - own,), jnp.float32)]
    ).reshape(8, 128)
    row_stats = lax.all_to_all(
        jnp.broadcast_to(row_message[None], (Z, 8, 128)), "z", 0, 0, tiled=True
    ).reshape(Z, 1024)

    stats = jnp.stack([col_top, col_total]).reshape(2, CORE, SIDE, SIDE, own)
    for place, axis, count in ((1, "core", CORE), (3, "x", SIDE), (2, "y", SIDE)):
        messages = [stats] + [
            jnp.roll(shift(stats, axis, count, by), by, axis=place) for by in range(1, count)
        ]
        messages = jnp.stack(messages)
        stats = jnp.stack(combine(messages[:, 0], messages[:, 1]))
    stats = stats.reshape(2, col_count)
    col_top, col_total = stats[0], stats[1]

    row_top, row_total = combine(row_stats[:, :row_count], row_stats[:, row_count:2 * row_count])
    row_targets = row_stats[:, 2 * row_count:2 * row_count + own].reshape(row_count).astype(jnp.int32)

    place = jnp.arange(col_count, dtype=jnp.int32)
    place_own, place = place % own, place // own
    place_x, place = (across - place % SIDE + SIDE) % SIDE, place // SIDE
    place_y, place = (along - place % SIDE + SIDE) % SIDE, place // SIDE
    place_core = (core - place + CORE) % CORE
    column_ids = (((plane * SIDE + place_x) * SIDE + place_y) * CORE + place_core) * own + place_own
    weights = (
        jnp.exp(scores - row_top[:, None]) * (0.5 / row_total)[:, None]
        + jnp.exp(scores - col_top[None, :]) * (0.5 / col_total)[None, :]
        - (row_targets[:, None] == column_ids[None, :]).astype(jnp.float32)
    )
    grad_rows = lax.dot_general(
        weights, cols, (((1,), (0,)), ((), ())),
        precision=lax.Precision.HIGH, preferred_element_type=jnp.float32,
    )
    row_parts = lax.all_to_all(grad_rows.reshape(Z, own, width), "z", 0, 0, tiled=True)
    grad_cols = lax.dot_general(
        weights, rows, (((0,), (0,)), ((), ())),
        precision=lax.Precision.HIGH, preferred_element_type=jnp.float32,
    ).reshape(CORE, SIDE, SIDE, own, width)
    col_sum = home(home(home(grad_cols, "core", CORE), "y", SIDE), "x", SIDE)
    return logit_scale * jnp.sum(row_parts, axis=0), logit_scale * col_sum


def solution(mesh):
    grid = Mesh(mesh.devices.reshape(Z, SIDE, SIDE, CORE), ALL)
    placed = P(ALL, None)
    return jax.shard_map(
        local, mesh=grid, in_specs=(placed, placed, P(), P(ALL)), out_specs=(placed, placed), check_vma=False
    )
```

```python
import jax
import jax.numpy as jnp
from jax import lax
from jax.sharding import Mesh, PartitionSpec as P

ALL = ("z", "x", "y", "core")
Z, SIDE, CORE = 16, 4, 2


def to_all(block, axes, count):
    sent = jnp.broadcast_to(block[None], (count,) + block.shape)
    return lax.all_to_all(sent, axes, 0, 0, tiled=True)


def shift(block, axis, count, by):
    return lax.ppermute(block, axis, [(i, (i + by) % count) for i in range(count)])


def home(parts, axis, count, dim, me):
    def part(by):
        return lax.dynamic_index_in_dim(parts, (me - by + count) % count, dim, keepdims=False)

    total = part(0)
    for by in range(1, count):
        total = total + shift(part(by), axis, count, -by)
    return total


def combine(tops, totals):
    top = jnp.max(tops, axis=0)
    return top, jnp.sum(totals * jnp.exp(tops - top[None]), axis=0)


def local(row_embed, col_embed, logit_scale, targets):
    own, width = row_embed.shape
    plane, across, along, core = (lax.axis_index(a) for a in ALL)
    other = shift(col_embed, "core", CORE, 1)
    pair = jnp.where(core == 0, jnp.concatenate([col_embed, other]), jnp.concatenate([other, col_embed]))
    cols = to_all(pair, ("x", "y"), SIDE * SIDE).reshape(SIDE * SIDE * CORE * own, width)
    rows = lax.all_gather(row_embed, "z", axis=0, tiled=True)
    row_count, col_count = rows.shape[0], cols.shape[0]

    scores = logit_scale * lax.dot_general(
        rows, cols, (((1,), (1,)), ((), ())),
        precision=lax.Precision.HIGHEST, preferred_element_type=jnp.float32,
    )
    row_top = jnp.max(scores, axis=1)
    row_total = jnp.sum(jnp.exp(scores - row_top[:, None]), axis=1)
    col_top = jnp.max(scores, axis=0)
    col_total = jnp.sum(jnp.exp(scores - col_top[None, :]), axis=0)

    row_message = jnp.concatenate(
        [row_top, row_total, targets.astype(jnp.float32), jnp.zeros((1024 - 2 * row_count - own,), jnp.float32)]
    ).reshape(8, 128)
    row_stats = to_all(row_message, "z", Z).reshape(Z, 1024)
    col_message = jnp.concatenate([col_top, col_total]).reshape(12, 128)
    col_stats = lax.all_gather(col_message, "x", axis=0).reshape(SIDE, 2, col_count)
    col_message = jnp.concatenate(combine(col_stats[:, 0], col_stats[:, 1])).reshape(12, 128)
    row_stats, col_message = lax.optimization_barrier((row_stats, col_message))
    col_stats = to_all(col_message, ("y", "core"), SIDE * CORE).reshape(SIDE * CORE, 2, col_count)
    col_top, col_total = combine(col_stats[:, 0], col_stats[:, 1])
    row_top, row_total = combine(row_stats[:, :row_count], row_stats[:, row_count:2 * row_count])
    row_targets = row_stats[:, 2 * row_count:2 * row_count + own].reshape(row_count).astype(jnp.int32)

    column_ids = plane * col_count + jnp.arange(col_count, dtype=jnp.int32)
    weights = (
        jnp.exp(scores - row_top[:, None]) * (0.5 / row_total)[:, None]
        + jnp.exp(scores - col_top[None, :]) * (0.5 / col_total)[None, :]
        - (row_targets[:, None] == column_ids[None, :]).astype(jnp.float32)
    )
    grad_rows = lax.dot_general(
        weights, cols, (((1,), (0,)), ((), ())),
        precision=lax.Precision.HIGH, preferred_element_type=jnp.float32,
    )
    row_parts = lax.all_to_all(grad_rows.reshape(Z, own, width), "z", 0, 0, tiled=True)
    grad_cols = lax.dot_general(
        weights, rows, (((0,), (0,)), ((), ())),
        precision=lax.Precision.HIGH, preferred_element_type=jnp.float32,
    ).reshape(SIDE, SIDE, CORE, own, width)
    col_sum = home(grad_cols, "core", CORE, 2, core)
    col_sum = home(col_sum, "y", SIDE, 1, along)
    col_sum = home(col_sum, "x", SIDE, 0, across)
    return logit_scale * jnp.sum(row_parts, axis=0), logit_scale * col_sum


def solution(mesh):
    grid = Mesh(mesh.devices.reshape(Z, SIDE, SIDE, CORE), ALL)
    placed = P(ALL, None)
    return jax.shard_map(
        local, mesh=grid, in_specs=(placed, placed, P(), P(ALL)), out_specs=(placed, placed), check_vma=False
    )
```

```python
import jax
import jax.numpy as jnp
from jax import lax
from jax.sharding import Mesh, PartitionSpec as P

ALL = ("z", "x", "y", "core")
Z, SIDE, CORE = 16, 4, 2
XY = SIDE * SIDE
SWAP = [(0, 1), (1, 0)]


def to_all(block, axes, count):
    sent = jnp.broadcast_to(block[None], (count,) + block.shape)
    return lax.all_to_all(sent, axes, 0, 0, tiled=True)


def log_sum_exp(values, axis):
    top = jnp.max(values, axis=axis, keepdims=True)
    return jnp.squeeze(top, axis) + jnp.log(jnp.sum(jnp.exp(values - top), axis=axis))


def local(row_embed, col_embed, logit_scale, targets):
    own, width = row_embed.shape
    plane, across, along, core = (lax.axis_index(a) for a in ALL)
    spot = (across * SIDE + along) * CORE + core
    targets = targets.astype(jnp.float32)

    mine = jnp.stack([col_embed, row_embed])
    other = lax.ppermute(mine, "core", SWAP)
    pair = jnp.where(core == 0, jnp.stack([mine, other], 1), jnp.stack([other, mine], 1))
    planes = to_all(pair, ("x", "y"), XY)
    planes = planes.transpose(1, 0, 2, 3, 4).reshape(2, XY * CORE * own, width)
    lines = lax.all_gather(jnp.stack([row_embed, col_embed]), "z", axis=1, tiled=True)
    line_count, plane_count = lines.shape[1], planes.shape[1]

    scores = logit_scale * lax.dot_general(
        lines, planes, (((2,), (2,)), ((0,), (0,))),
        precision=lax.Precision.HIGHEST, preferred_element_type=jnp.float32,
    )

    message = jnp.concatenate([log_sum_exp(scores, 1).reshape(2 * plane_count), targets])
    message = jnp.pad(message, (0, 16 * 128 - message.shape[0])).reshape(16, 128)
    heard = to_all(message, ("x", "y", "core"), XY * CORE).reshape(XY * CORE, 16 * 128)
    plane_lse = log_sum_exp(heard[:, :2 * plane_count], 0).reshape(2, plane_count)
    plane_targets = heard[:, 2 * plane_count:2 * plane_count + own].reshape(plane_count)

    own_lse = lax.dynamic_slice(plane_lse, (0, spot * own), (2, own))
    message = jnp.pad(jnp.concatenate([own_lse[1], own_lse[0], targets]), (0, 128 - 3 * own)).reshape(1, 128)
    heard = to_all(message, "z", Z).reshape(Z, 128)
    line_lse = heard[:, :2 * own].reshape(Z, 2, own).transpose(1, 0, 2).reshape(2, line_count)
    line_targets = heard[:, 2 * own:3 * own].reshape(line_count)

    numbers = jnp.arange(own)
    plane_ids = (plane * plane_count + jnp.arange(plane_count)).astype(jnp.float32)
    line_ids = ((jnp.arange(Z)[:, None] * (XY * CORE) + spot) * own + numbers[None, :]).reshape(line_count)
    line_key = jnp.stack([line_targets, line_ids.astype(jnp.float32)])
    plane_key = jnp.stack([plane_ids, plane_targets])
    weights = (
        0.5 * jnp.exp(scores - line_lse[:, :, None])
        + 0.5 * jnp.exp(scores - plane_lse[:, None, :])
        - (line_key[:, :, None] == plane_key[:, None, :]).astype(jnp.float32)
    )
    grads = lax.dot_general(
        weights, lines, (((1,), (1,)), ((0,), (0,))),
        precision=lax.Precision.HIGH, preferred_element_type=jnp.float32,
    ).reshape(2, XY, CORE, own, width)
    kept = lax.dynamic_index_in_dim(grads, core, 2, keepdims=False)
    given = lax.dynamic_index_in_dim(grads, 1 - core, 2, keepdims=False)
    parts = (kept + lax.ppermute(given, "core", SWAP)).transpose(1, 0, 2, 3)
    parts = lax.all_to_all(parts, ("x", "y"), 0, 0, tiled=True)
    total = logit_scale * jnp.sum(parts, axis=0)
    return total[1], total[0]


def solution(mesh):
    grid = Mesh(mesh.devices.reshape(Z, SIDE, SIDE, CORE), ALL)
    placed = P(ALL, None)
    return jax.shard_map(
        local, mesh=grid, in_specs=(placed, placed, P(), P(ALL)), out_specs=(placed, placed), check_vma=False
    )
```

```python
import jax
import jax.numpy as jnp
from jax import lax
from jax.experimental import pallas as pl
from jax.experimental.pallas import tpu as pltpu
from jax.sharding import Mesh, PartitionSpec as P

ALL = ("far", "pair", "x", "y", "core")
FAR, PAIR, SIDE, CORE = 8, 2, 4, 2
Z, XY = FAR * PAIR, SIDE * SIDE
SWAP = [(0, 1), (1, 0)]
VMEM = pl.BlockSpec(memory_space=pltpu.VMEM)
PARAMS = pltpu.CompilerParams(vmem_limit_bytes=48 * 1024 * 1024)


def to_all(block, axes, count):
    sent = jnp.broadcast_to(block[None], (count,) + block.shape)
    return lax.all_to_all(sent, axes, 0, 0, tiled=True)


def log_sum_exp(values, axis):
    top = jnp.max(values, axis=axis, keepdims=True)
    return jnp.squeeze(top, axis) + jnp.log(jnp.sum(jnp.exp(values - top), axis=axis))


def flat(ref, which):
    block = ref[:, which]
    return block.reshape(block.shape[0] * block.shape[1], block.shape[2])


def score_kernel(scale_ref, line0_ref, line1_ref, near_ref, far_ref, near_out, far_out, lse_out):
    scale = scale_ref[0]
    half = near_out.shape[1] // 2
    for side, (plane_ref, out) in enumerate(((near_ref, near_out), (far_ref, far_out))):
        for b in range(2):
            plane = flat(plane_ref, b)
            tops = []
            for k, line_ref in enumerate((line0_ref, line1_ref)):
                block = scale * lax.dot_general(
                    flat(line_ref, 1 - b), plane, (((1,), (1,)), ((), ())),
                    precision=lax.Precision.HIGHEST, preferred_element_type=jnp.float32,
                )
                out[b, k * half:(k + 1) * half, :] = block
                tops.append(jnp.max(block, axis=0, keepdims=True))
            top = jnp.maximum(tops[0], tops[1])
            total = jnp.sum(jnp.exp(out[b] - top), axis=0, keepdims=True)
            row = side * 2 + b
            lse_out[row:row + 1, :] = top + jnp.log(total)


def split(values):
    high = values.astype(jnp.bfloat16)
    return high, (values - high.astype(jnp.float32)).astype(jnp.bfloat16)


def upright(row):
    return jnp.transpose(jnp.broadcast_to(row, (128, row.shape[1])))[:, :1]


def grad_kernel(scale_ref, score_ref, line0_ref, line1_ref, line_ref, plane_ref, out):
    scale = scale_ref[0]
    count = score_ref.shape[1]
    for b in range(2):
        scores = score_ref[b]
        line_lse, line_key = upright(line_ref[b:b + 1, :]), upright(line_ref[2 + b:3 + b, :])
        plane_lse, plane_key = plane_ref[b:b + 1, :], plane_ref[2 + b:3 + b, :]
        weights = (
            0.5 * jnp.exp(scores - line_lse)
            + 0.5 * jnp.exp(scores - plane_lse)
            - jnp.where(line_key == plane_key, 1.0, 0.0)
        )
        total = None
        for k, ref in enumerate((line0_ref, line1_ref)):
            high, low = split(weights[k * count // 2:(k + 1) * count // 2])
            line_high, line_low = split(flat(ref, 1 - b))
            for left, right in ((high, line_high), (high, line_low), (low, line_high)):
                term = lax.dot_general(
                    left, right, (((0,), (0,)), ((), ())), preferred_element_type=jnp.float32
                )
                total = term if total is None else total + term
        out[:, b] = (scale * total).reshape(out.shape[0], out.shape[2], out.shape[3])


def local(row_embed, col_embed, logit_scale, targets):
    own, width = row_embed.shape
    far, pair, across, along, core = (lax.axis_index(a) for a in ALL)
    chip = across * SIDE + along
    spot = chip * CORE + core
    scale = logit_scale.reshape(1)
    targets = targets.astype(jnp.float32)
    line_count, plane_count = Z * own, XY * own

    def mine_first(first, second, me):
        return jnp.where(me == 0, first, second), jnp.where(me == 0, second, first)

    mine = jnp.stack([col_embed, row_embed])
    near = to_all(mine, ("x", "y"), XY)
    line0 = lax.all_gather(mine, "far", axis=0)
    line1 = lax.ppermute(line0, "pair", SWAP)
    away = lax.ppermute(near, "core", SWAP)

    smem = pl.BlockSpec(memory_space=pltpu.SMEM)
    block = jax.ShapeDtypeStruct((2, line_count, plane_count), jnp.float32)
    near_scores, away_scores, lse = pl.pallas_call(
        score_kernel,
        out_shape=(block, block, jax.ShapeDtypeStruct((4, plane_count), jnp.float32)),
        in_specs=[smem, VMEM, VMEM, VMEM, VMEM],
        out_specs=(VMEM, VMEM, VMEM),
        compiler_params=PARAMS,
        name="scores",
    )(scale, line0, line1, near, away)

    message = jnp.concatenate(mine_first(lse[:2], lse[2:], core)).reshape(4 * plane_count)
    message = jnp.concatenate([message, targets])
    message = jnp.pad(message, (0, 16 * 128 - message.shape[0])).reshape(16, 128)
    heard = to_all(message, ("x", "y", "core"), XY * CORE).reshape(XY * CORE, 16 * 128)
    plane_lse = log_sum_exp(heard[:, :4 * plane_count], 0).reshape(CORE, 2, plane_count)
    plane_targets = heard[:, 4 * plane_count:4 * plane_count + own].reshape(XY, CORE, own)
    plane_targets = plane_targets.transpose(1, 0, 2).reshape(CORE, plane_count)
    near_lse, away_lse = mine_first(plane_lse[0], plane_lse[1], core)
    near_targets, away_targets = mine_first(plane_targets[0], plane_targets[1], core)

    own_lse = lax.dynamic_slice(near_lse, (0, chip * own), (2, own)).reshape(2 * own)
    message = jnp.pad(jnp.concatenate([own_lse, targets]), (0, 128 - 3 * own)).reshape(1, 128)
    heard = to_all(message, ("far", "pair"), Z).reshape(FAR, PAIR, 128)[:, :, :3 * own].reshape(FAR, PAIR, 3, own)
    heard = jnp.stack(mine_first(heard[:, 0], heard[:, 1], pair)).transpose(2, 0, 1, 3).reshape(3, line_count)

    numbers = jnp.arange(own)
    line_z = jnp.arange(FAR)[None, :] * PAIR + jnp.stack([pair, 1 - pair])[:, None]
    line_ids = ((line_z[:, :, None] * (XY * CORE) + spot) * own + numbers).reshape(line_count).astype(jnp.float32)
    line_info = jnp.stack([heard[1], heard[0], heard[2], line_ids])

    def plane_info(plane_lse, plane_targets, which):
        ids = (((far * PAIR + pair) * XY + jnp.arange(XY)[:, None]) * CORE + which) * own + numbers[None, :]
        ids = ids.reshape(1, plane_count).astype(jnp.float32)
        return jnp.concatenate([plane_lse, ids, plane_targets[None]])

    def grads(scores, info):
        return pl.pallas_call(
            grad_kernel,
            out_shape=jax.ShapeDtypeStruct((XY, 2, own, width), jnp.float32),
            in_specs=[smem, VMEM, VMEM, VMEM, VMEM, VMEM],
            out_specs=VMEM,
            compiler_params=PARAMS,
            name="grads",
        )(scale, scores, line0, line1, line_info, info)

    given = grads(away_scores, plane_info(away_lse, away_targets, 1 - core))
    taken = lax.ppermute(given, "core", SWAP)
    parts = grads(near_scores, plane_info(near_lse, near_targets, core)) + taken
    total = jnp.sum(lax.all_to_all(parts, ("x", "y"), 0, 0, tiled=True), axis=0)
    return total[1], total[0]


def solution(mesh):
    grid = Mesh(mesh.devices.reshape(FAR, PAIR, SIDE, SIDE, CORE), ALL)
    placed = P(ALL, None)
    return jax.shard_map(
        local, mesh=grid, in_specs=(placed, placed, P(), P(ALL)), out_specs=(placed, placed), check_vma=False
    )
```

```python
import jax
import jax.numpy as jnp
from jax import lax
from jax.sharding import Mesh, PartitionSpec as P

ALL = ("z", "x", "y", "core")
Z, SIDE, CORE = 16, 4, 2


def to_all(block, axes, count):
    sent = jnp.broadcast_to(block[None], (count,) + block.shape)
    return lax.all_to_all(sent, axes, 0, 0, tiled=True)


def shift(block, axis, count, by):
    return lax.ppermute(block, axis, [(i, (i + by) % count) for i in range(count)])


def home(parts, axis, count, dim, me):
    def part(by):
        return lax.dynamic_index_in_dim(parts, (me - by + count) % count, dim, keepdims=False)

    total = part(0)
    for by in range(1, count):
        total = total + shift(part(by), axis, count, -by)
    return total


def combine(tops, totals):
    top = jnp.max(tops, axis=0)
    return top, jnp.sum(totals * jnp.exp(tops - top[None]), axis=0)


def local(row_embed, col_embed, logit_scale, targets):
    own, width = row_embed.shape
    plane, across, along, core = (lax.axis_index(a) for a in ALL)
    cols = to_all(col_embed, ("x", "y", "core"), SIDE * SIDE * CORE).reshape(SIDE * SIDE * CORE * own, width)
    rows = lax.all_gather(row_embed, "z", axis=0, tiled=True)
    row_count, col_count = rows.shape[0], cols.shape[0]

    scores = logit_scale * lax.dot_general(
        rows, cols, (((1,), (1,)), ((), ())),
        precision=lax.Precision.HIGHEST, preferred_element_type=jnp.float32,
    )
    row_top = jnp.max(scores, axis=1)
    row_total = jnp.sum(jnp.exp(scores - row_top[:, None]), axis=1)
    col_top = jnp.max(scores, axis=0)
    col_total = jnp.sum(jnp.exp(scores - col_top[None, :]), axis=0)

    row_message = jnp.concatenate(
        [row_top, row_total, targets.astype(jnp.float32), jnp.zeros((1024 - 2 * row_count - own,), jnp.float32)]
    ).reshape(8, 128)
    col_message = jnp.concatenate([col_top, col_total]).reshape(12, 128)
    col_stats = to_all(col_message, ("x", "y", "core"), SIDE * SIDE * CORE)
    col_stats, row_message = lax.optimization_barrier((col_stats, row_message))
    row_stats = to_all(row_message, "z", Z).reshape(Z, 1024)
    col_stats = col_stats.reshape(SIDE * SIDE * CORE, 2, col_count)
    col_top, col_total = combine(col_stats[:, 0], col_stats[:, 1])
    row_top, row_total = combine(row_stats[:, :row_count], row_stats[:, row_count:2 * row_count])
    row_targets = row_stats[:, 2 * row_count:2 * row_count + own].reshape(row_count).astype(jnp.int32)

    column_ids = plane * col_count + jnp.arange(col_count, dtype=jnp.int32)
    weights = (
        jnp.exp(scores - row_top[:, None]) * (0.5 / row_total)[:, None]
        + jnp.exp(scores - col_top[None, :]) * (0.5 / col_total)[None, :]
        - (row_targets[:, None] == column_ids[None, :]).astype(jnp.float32)
    )
    grad_rows = lax.dot_general(
        weights, cols, (((1,), (0,)), ((), ())),
        precision=lax.Precision.HIGH, preferred_element_type=jnp.float32,
    )
    row_parts = lax.all_to_all(grad_rows.reshape(Z, own, width), "z", 0, 0, tiled=True)
    grad_cols = lax.dot_general(
        weights, rows, (((0,), (0,)), ((), ())),
        precision=lax.Precision.HIGH, preferred_element_type=jnp.float32,
    ).reshape(SIDE, SIDE, CORE, own, width)
    col_sum = home(grad_cols, "core", CORE, 2, core)
    col_sum = home(col_sum, "y", SIDE, 1, along)
    col_sum = home(col_sum, "x", SIDE, 0, across)
    return logit_scale * jnp.sum(row_parts, axis=0), logit_scale * col_sum


def solution(mesh):
    grid = Mesh(mesh.devices.reshape(Z, SIDE, SIDE, CORE), ALL)
    placed = P(ALL, None)
    return jax.shard_map(
        local, mesh=grid, in_specs=(placed, placed, P(), P(ALL)), out_specs=(placed, placed), check_vma=False
    )
```

```python
import jax
import jax.numpy as jnp
from jax import lax
from jax.experimental import pallas as pl
from jax.experimental.pallas import tpu as pltpu
from jax.sharding import Mesh, PartitionSpec as P

ALL = ("z", "x", "y", "core")
Z, SIDE, CORE = 16, 4, 2
PLANE = SIDE * SIDE * CORE
LANES = 128
SMEM = pl.BlockSpec(memory_space=pltpu.SMEM)
VMEM = pl.BlockSpec(memory_space=pltpu.VMEM)
PARAMS = pltpu.CompilerParams(vmem_limit_bytes=48 * 1024 * 1024)


def to_all(block, axes, count):
    sent = jnp.broadcast_to(block[None], (count,) + block.shape)
    return lax.all_to_all(sent, axes, 0, 0, tiled=True)


def shift(block, axis, count, by):
    return lax.ppermute(block, axis, [(i, (i + by) % count) for i in range(count)])


def home(parts, axis, count, dim, me):
    def part(by):
        return lax.dynamic_index_in_dim(parts, (me - by + count) % count, dim, keepdims=False)

    total = part(0)
    for by in range(1, count):
        total = total + shift(part(by), axis, count, -by)
    return total


def score_kernel(scale_ref, row_ref, col_ref, target_ref, score_out, col_out, row_out):
    scores = scale_ref[0] * lax.dot_general(
        row_ref[...], col_ref[...], (((1,), (1,)), ((), ())),
        precision=lax.Precision.HIGHEST, preferred_element_type=jnp.float32,
    )
    score_out[...] = scores
    top = jnp.max(scores, axis=0, keepdims=True)
    lse = top + jnp.log(jnp.sum(jnp.exp(scores - top), axis=0, keepdims=True))
    used = lse.shape[1] // LANES
    for k in range(used):
        col_out[:, k, :] = jnp.broadcast_to(lse[:, k * LANES:(k + 1) * LANES], (col_out.shape[0], LANES))
    col_out[:, used:, :] = jnp.zeros_like(col_out[:, used:, :])
    used = score_out.shape[0] // LANES
    for k in range(used):
        part = scores[k * LANES:(k + 1) * LANES]
        top = jnp.max(part, axis=1, keepdims=True)
        lse = top + jnp.log(jnp.sum(jnp.exp(part - top), axis=1, keepdims=True))
        lse = jnp.transpose(jnp.broadcast_to(lse, (LANES, LANES)))[:1]
        row_out[:, k, :] = jnp.broadcast_to(lse, (row_out.shape[0], LANES))
    row_out[:, used, :] = jnp.broadcast_to(target_ref[...], (row_out.shape[0], LANES))
    row_out[:, used + 1:, :] = jnp.zeros_like(row_out[:, used + 1:, :])


def split(values):
    high = values.astype(jnp.bfloat16)
    return high, (values - high.astype(jnp.float32)).astype(jnp.bfloat16)


def combined(heard):
    top = jnp.max(heard, axis=0)
    return top + jnp.log(jnp.sum(jnp.exp(heard - top[None]), axis=0))


def weight_kernel(scale_ref, base_ref, score_ref, col_ref, heard_col_ref, heard_row_ref, weight_out, grad_out):
    row_count, col_count = score_ref.shape
    own = grad_out.shape[1]
    col_lse = combined(heard_col_ref[...])
    col_lse = jnp.concatenate([col_lse[k:k + 1] for k in range(col_count // LANES)], axis=1)
    row_lse = combined(heard_row_ref[...])
    row_lse = jnp.concatenate(
        [jnp.transpose(jnp.broadcast_to(row_lse[k:k + 1], (LANES, LANES))) for k in range(row_count // LANES)], axis=0
    )[:, :1]
    targets = jnp.transpose(
        jnp.concatenate([heard_row_ref[:, row_count // LANES, :], jnp.zeros((LANES - Z, LANES), jnp.float32)], axis=0)
    )
    ids = lax.broadcasted_iota(jnp.int32, (own, col_count), 1).astype(jnp.float32)
    base = base_ref[0]
    for z in range(Z):
        here = slice(z * own, (z + 1) * own)
        scores = score_ref[here, :]
        weight_out[here, :] = (
            0.5 * jnp.exp(scores - row_lse[here])
            + 0.5 * jnp.exp(scores - col_lse)
            - jnp.where(targets[:own, z:z + 1] - base == ids, 1.0, 0.0)
        )
    high, low = split(weight_out[...])
    col_high, col_low = split(col_ref[...])
    total = None
    for left, right in ((high, col_high), (high, col_low), (low, col_high)):
        term = jnp.dot(left, right, preferred_element_type=jnp.float32)
        total = term if total is None else total + term
    grad_out[...] = (scale_ref[0] * total).reshape(grad_out.shape)


def local(row_embed, col_embed, logit_scale, targets):
    own, width = row_embed.shape
    plane, across, along, core = (lax.axis_index(a) for a in ALL)
    scale = logit_scale.reshape(1)
    cols = to_all(col_embed, ("x", "y", "core"), PLANE).reshape(PLANE * own, width)
    rows = lax.all_gather(row_embed, "z", axis=0, tiled=True)
    row_count, col_count = rows.shape[0], cols.shape[0]

    numbers = jnp.pad(targets.astype(jnp.float32), (0, LANES - own)).reshape(1, LANES)
    scores, col_message, row_message = pl.pallas_call(
        score_kernel,
        out_shape=(
            jax.ShapeDtypeStruct((row_count, col_count), jnp.float32),
            jax.ShapeDtypeStruct((PLANE, 8, LANES), jnp.float32),
            jax.ShapeDtypeStruct((Z, 8, LANES), jnp.float32),
        ),
        in_specs=[SMEM, VMEM, VMEM, VMEM],
        out_specs=(VMEM, VMEM, VMEM),
        compiler_params=PARAMS,
        name="scores",
    )(scale, rows, cols, numbers)

    heard_col = lax.all_to_all(col_message, ("x", "y", "core"), 0, 0, tiled=True)
    heard_col, row_message = lax.optimization_barrier((heard_col, row_message))
    heard_row = lax.all_to_all(row_message, "z", 0, 0, tiled=True)

    weights, grad_rows = pl.pallas_call(
        weight_kernel,
        out_shape=(
            jax.ShapeDtypeStruct((row_count, col_count), jnp.float32),
            jax.ShapeDtypeStruct((Z, own, width), jnp.float32),
        ),
        in_specs=[SMEM, SMEM, VMEM, VMEM, VMEM, VMEM],
        out_specs=(VMEM, VMEM),
        compiler_params=PARAMS,
        name="weights",
    )(scale, (plane * col_count).astype(jnp.float32).reshape(1), scores, cols, heard_col, heard_row)
    row_parts = lax.all_to_all(grad_rows, "z", 0, 0, tiled=True)
    grad_cols = lax.dot_general(
        weights, rows, (((0,), (0,)), ((), ())),
        precision=lax.Precision.HIGH, preferred_element_type=jnp.float32,
    ).reshape(SIDE, SIDE, CORE, own, width)
    col_sum = home(grad_cols, "core", CORE, 2, core)
    col_sum = home(col_sum, "y", SIDE, 1, along)
    col_sum = home(col_sum, "x", SIDE, 0, across)
    return jnp.sum(row_parts, axis=0), logit_scale * col_sum


def solution(mesh):
    grid = Mesh(mesh.devices.reshape(Z, SIDE, SIDE, CORE), ALL)
    placed = P(ALL, None)
    return jax.shard_map(
        local, mesh=grid, in_specs=(placed, placed, P(), P(ALL)), out_specs=(placed, placed), check_vma=False
    )
```

```python
import jax
import jax.numpy as jnp
from jax import lax
from jax.experimental import pallas as pl
from jax.experimental.pallas import tpu as pltpu
from jax.sharding import Mesh, PartitionSpec as P

ALL = ("z", "x", "y", "core")
Z, SIDE, CORE = 16, 4, 2
PLANE = SIDE * SIDE * CORE
LANES = 128
SMEM = pl.BlockSpec(memory_space=pltpu.SMEM)
VMEM = pl.BlockSpec(memory_space=pltpu.VMEM)
ANY = pl.BlockSpec(memory_space=pl.ANY)
HBM = pl.BlockSpec(memory_space=pltpu.HBM)
PARAMS = pltpu.CompilerParams(vmem_limit_bytes=48 * 1024 * 1024)


def to_all(block, axes, count):
    sent = jnp.broadcast_to(block[None], (count,) + block.shape)
    return lax.all_to_all(sent, axes, 0, 0, tiled=True)


def shift(block, axis, count, by):
    return lax.ppermute(block, axis, [(i, (i + by) % count) for i in range(count)])


def home(parts, axis, count, dim, me):
    def part(by):
        return lax.dynamic_index_in_dim(parts, (me - by + count) % count, dim, keepdims=False)

    total = part(0)
    for by in range(1, count):
        total = total + shift(part(by), axis, count, -by)
    return total


def score_kernel(
    scale_ref, row_ref, col_ref, target_ref, score_out, col_out, row_out, score_ref, col_part, row_part, sems
):
    stores = [
        pltpu.make_async_copy(source, target, sems.at[k])
        for k, (source, target) in enumerate(((score_ref, score_out), (row_part, row_out), (col_part, col_out)))
    ]
    scores = scale_ref[0] * lax.dot_general(
        row_ref[...], col_ref[...], (((1,), (1,)), ((), ())),
        precision=lax.Precision.HIGHEST, preferred_element_type=jnp.float32,
    )
    score_ref[...] = scores
    stores[0].start()
    used = scores.shape[0] // LANES
    for k in range(used):
        part = scores[k * LANES:(k + 1) * LANES]
        top = jnp.max(part, axis=1, keepdims=True)
        lse = top + jnp.log(jnp.sum(jnp.exp(part - top), axis=1, keepdims=True))
        lse = jnp.transpose(jnp.broadcast_to(lse, (LANES, LANES)))[:1]
        row_part[:, k, :] = jnp.broadcast_to(lse, (row_part.shape[0], LANES))
    row_part[:, used, :] = jnp.broadcast_to(target_ref[...], (row_part.shape[0], LANES))
    row_part[:, used + 1:, :] = jnp.zeros_like(row_part[:, used + 1:, :])
    stores[1].start()
    top = jnp.max(scores, axis=0, keepdims=True)
    lse = top + jnp.log(jnp.sum(jnp.exp(scores - top), axis=0, keepdims=True))
    used = lse.shape[1] // LANES
    for k in range(used):
        col_part[:, k, :] = jnp.broadcast_to(lse[:, k * LANES:(k + 1) * LANES], (col_part.shape[0], LANES))
    col_part[:, used:, :] = jnp.zeros_like(col_part[:, used:, :])
    stores[2].start()
    for store in stores:
        store.wait()


def split(values):
    high = values.astype(jnp.bfloat16)
    return high, (values - high.astype(jnp.float32)).astype(jnp.bfloat16)


def combined(heard):
    top = jnp.max(heard, axis=0)
    return top + jnp.log(jnp.sum(jnp.exp(heard - top[None]), axis=0))


def weight_kernel(
    scale_ref, base_ref, col_ref, score_in, heard_col_in, heard_row_in,
    weight_out, grad_out, score_ref, heard_col_ref, heard_row_ref, weight_ref, grad_ref, sems, out_sems,
):
    fetches = [
        pltpu.make_async_copy(source, target, sems.at[k])
        for k, (source, target) in enumerate(
            ((heard_row_in, heard_row_ref), (heard_col_in, heard_col_ref), (score_in, score_ref))
        )
    ]
    for fetch in fetches:
        fetch.start()
    row_count, col_count = score_ref.shape
    own = grad_ref.shape[1]
    col_high, col_low = split(col_ref[...])
    ids = lax.broadcasted_iota(jnp.int32, (own, col_count), 1).astype(jnp.float32)
    base = base_ref[0]
    for fetch in fetches:
        fetch.wait()
    col_lse = combined(heard_col_ref[...])
    col_lse = jnp.concatenate([col_lse[k:k + 1] for k in range(col_count // LANES)], axis=1)
    row_lse = combined(heard_row_ref[...])
    row_lse = jnp.concatenate(
        [jnp.transpose(jnp.broadcast_to(row_lse[k:k + 1], (LANES, LANES))) for k in range(row_count // LANES)], axis=0
    )[:, :1]
    targets = jnp.transpose(
        jnp.concatenate([heard_row_ref[:, row_count // LANES, :], jnp.zeros((LANES - Z, LANES), jnp.float32)], axis=0)
    )
    stores = []
    for part in range(2):
        first, count = part * Z // 2, Z // 2
        for z in range(first, first + count):
            here = slice(z * own, (z + 1) * own)
            scores = score_ref[here, :]
            weight_ref[here, :] = (
                0.5 * jnp.exp(scores - row_lse[here])
                + 0.5 * jnp.exp(scores - col_lse)
                - jnp.where(targets[:own, z:z + 1] - base == ids, 1.0, 0.0)
            )
        here = pl.ds(first * own, count * own)
        stores.append(pltpu.make_async_copy(weight_ref.at[here], weight_out.at[here], out_sems.at[0, part]))
        stores[-1].start()
        high, low = split(weight_ref[first * own:(first + count) * own, :])
        total = None
        for left, right in ((high, col_high), (high, col_low), (low, col_high)):
            term = jnp.dot(left, right, preferred_element_type=jnp.float32)
            total = term if total is None else total + term
        here = pl.ds(first, count)
        grad_ref[here] = (scale_ref[0] * total).reshape(count, own, total.shape[1])
        stores.append(pltpu.make_async_copy(grad_ref.at[here], grad_out.at[here], out_sems.at[1, part]))
        stores[-1].start()
    for store in stores:
        store.wait()


def local(row_embed, col_embed, logit_scale, targets):
    own, width = row_embed.shape
    plane, across, along, core = (lax.axis_index(a) for a in ALL)
    scale = logit_scale.reshape(1)
    cols = to_all(col_embed, ("x", "y", "core"), PLANE).reshape(PLANE * own, width)
    rows = lax.all_gather(row_embed, "z", axis=0, tiled=True)
    row_count, col_count = rows.shape[0], cols.shape[0]

    numbers = jnp.pad(targets.astype(jnp.float32), (0, LANES - own)).reshape(1, LANES)
    scores, col_message, row_message = pl.pallas_call(
        score_kernel,
        out_shape=(
            jax.ShapeDtypeStruct((row_count, col_count), jnp.float32),
            pltpu.HBM((SIDE * CORE, 8, LANES), jnp.float32),
            pltpu.HBM((Z, 8, LANES), jnp.float32),
        ),
        in_specs=[SMEM, VMEM, VMEM, VMEM],
        out_specs=(ANY, HBM, HBM),
        scratch_shapes=[
            pltpu.VMEM((row_count, col_count), jnp.float32),
            pltpu.VMEM((SIDE * CORE, 8, LANES), jnp.float32),
            pltpu.VMEM((Z, 8, LANES), jnp.float32),
            pltpu.SemaphoreType.DMA((3,)),
        ],
        compiler_params=PARAMS,
        name="scores",
    )(scale, rows, cols, numbers)

    heard_col = lax.all_to_all(col_message, ("y", "core"), 0, 0, tiled=True)
    heard_col, row_message = lax.optimization_barrier((heard_col, row_message))
    top = jnp.max(heard_col, axis=0)
    heard_col = lax.all_gather(top + jnp.log(jnp.sum(jnp.exp(heard_col - top[None]), axis=0)), "x", axis=0)
    heard_row = lax.all_to_all(row_message, "z", 0, 0, tiled=True)

    weights, grad_rows = pl.pallas_call(
        weight_kernel,
        out_shape=(
            pltpu.HBM((row_count, col_count), jnp.float32),
            pltpu.HBM((Z, own, width), jnp.float32),
        ),
        in_specs=[SMEM, SMEM, VMEM, ANY, ANY, ANY],
        out_specs=(HBM, HBM),
        scratch_shapes=[
            pltpu.VMEM((row_count, col_count), jnp.float32),
            pltpu.VMEM((SIDE, 8, LANES), jnp.float32),
            pltpu.VMEM((Z, 8, LANES), jnp.float32),
            pltpu.VMEM((row_count, col_count), jnp.float32),
            pltpu.VMEM((Z, own, width), jnp.float32),
            pltpu.SemaphoreType.DMA((3,)),
            pltpu.SemaphoreType.DMA((2, 2)),
        ],
        compiler_params=PARAMS,
        name="weights",
    )(scale, (plane * col_count).astype(jnp.float32).reshape(1), cols, scores, heard_col, heard_row)
    row_parts = lax.all_to_all(grad_rows, "z", 0, 0, tiled=True)
    grad_cols = lax.dot_general(
        weights, rows, (((0,), (0,)), ((), ())),
        precision=lax.Precision.HIGH, preferred_element_type=jnp.float32,
    ).reshape(SIDE, SIDE, CORE, own, width)
    col_sum = home(grad_cols, "core", CORE, 2, core)
    col_sum = home(col_sum, "y", SIDE, 1, along)
    col_sum = home(col_sum, "x", SIDE, 0, across)
    return jnp.sum(row_parts, axis=0), logit_scale * col_sum


def solution(mesh):
    grid = Mesh(mesh.devices.reshape(Z, SIDE, SIDE, CORE), ALL)
    placed = P(ALL, None)
    return jax.shard_map(
        local, mesh=grid, in_specs=(placed, placed, P(), P(ALL)), out_specs=(placed, placed), check_vma=False
    )
```

```python
import jax
import jax.numpy as jnp
from jax import lax
from jax.experimental import pallas as pl
from jax.experimental.pallas import tpu as pltpu
from jax.sharding import Mesh, PartitionSpec as P

ALL = ("z", "x", "y", "core")
Z, SIDE, CORE = 16, 4, 2
PLANE = SIDE * SIDE * CORE
LANES = 128
SMEM = pl.BlockSpec(memory_space=pltpu.SMEM)
VMEM = pl.BlockSpec(memory_space=pltpu.VMEM)
ANY = pl.BlockSpec(memory_space=pl.ANY)
HBM = pl.BlockSpec(memory_space=pltpu.HBM)
PARAMS = pltpu.CompilerParams(vmem_limit_bytes=48 * 1024 * 1024)


def to_all(block, axes, count):
    sent = jnp.broadcast_to(block[None], (count,) + block.shape)
    return lax.all_to_all(sent, axes, 0, 0, tiled=True)


def shift(block, axis, count, by):
    return lax.ppermute(block, axis, [(i, (i + by) % count) for i in range(count)])


def home(parts, axis, count, dim, me):
    def part(by):
        return lax.dynamic_index_in_dim(parts, (me - by + count) % count, dim, keepdims=False)

    total = part(0)
    for by in range(1, count):
        total = total + shift(part(by), axis, count, -by)
    return total


def score_kernel(
    scale_ref, row_ref, col_ref, target_ref, score_out, col_out, row_out, score_ref, col_part, row_part, sems
):
    stores = [
        pltpu.make_async_copy(source, target, sems.at[k])
        for k, (source, target) in enumerate(((score_ref, score_out), (row_part, row_out), (col_part, col_out)))
    ]
    scores = scale_ref[0] * lax.dot_general(
        row_ref[...], col_ref[...], (((1,), (1,)), ((), ())),
        precision=lax.Precision.HIGHEST, preferred_element_type=jnp.float32,
    )
    score_ref[...] = scores
    stores[0].start()
    used = scores.shape[0] // LANES
    for k in range(used):
        part = scores[k * LANES:(k + 1) * LANES]
        top = jnp.max(part, axis=1, keepdims=True)
        lse = top + jnp.log(jnp.sum(jnp.exp(part - top), axis=1, keepdims=True))
        lse = jnp.transpose(jnp.broadcast_to(lse, (LANES, LANES)))[:1]
        row_part[:, k, :] = jnp.broadcast_to(lse, (row_part.shape[0], LANES))
    row_part[:, used, :] = jnp.broadcast_to(target_ref[...], (row_part.shape[0], LANES))
    row_part[:, used + 1:, :] = jnp.zeros_like(row_part[:, used + 1:, :])
    stores[1].start()
    top = jnp.max(scores, axis=0, keepdims=True)
    lse = top + jnp.log(jnp.sum(jnp.exp(scores - top), axis=0, keepdims=True))
    used = lse.shape[1] // LANES
    for k in range(used):
        col_part[:, k, :] = jnp.broadcast_to(lse[:, k * LANES:(k + 1) * LANES], (col_part.shape[0], LANES))
    col_part[:, used:, :] = jnp.zeros_like(col_part[:, used:, :])
    stores[2].start()
    for store in stores:
        store.wait()


def split(values):
    high = values.astype(jnp.bfloat16)
    return high, (values - high.astype(jnp.float32)).astype(jnp.bfloat16)


def combined(heard):
    top = jnp.max(heard, axis=0)
    return top + jnp.log(jnp.sum(jnp.exp(heard - top[None]), axis=0))


def weight_kernel(
    scale_ref, base_ref, col_ref, score_in, heard_col_in, heard_row_in,
    weight_out, grad_out, score_ref, heard_col_ref, heard_row_ref, weight_ref, grad_ref, sems, out_sems,
):
    fetches = [
        pltpu.make_async_copy(source, target, sems.at[k])
        for k, (source, target) in enumerate(
            ((heard_row_in, heard_row_ref), (heard_col_in, heard_col_ref), (score_in, score_ref))
        )
    ]
    for fetch in fetches:
        fetch.start()
    row_count, col_count = score_ref.shape
    own = grad_ref.shape[1]
    col_high, col_low = split(col_ref[...])
    ids = lax.broadcasted_iota(jnp.int32, (own, col_count), 1).astype(jnp.float32)
    base = base_ref[0]
    for fetch in fetches:
        fetch.wait()
    col_lse = combined(heard_col_ref[...])
    col_lse = jnp.concatenate([col_lse[k:k + 1] for k in range(col_count // LANES)], axis=1)
    row_lse = combined(heard_row_ref[...])
    row_lse = jnp.concatenate(
        [jnp.transpose(jnp.broadcast_to(row_lse[k:k + 1], (LANES, LANES))) for k in range(row_count // LANES)], axis=0
    )[:, :1]
    targets = jnp.transpose(
        jnp.concatenate([heard_row_ref[:, row_count // LANES, :], jnp.zeros((LANES - Z, LANES), jnp.float32)], axis=0)
    )
    stores = []
    for part in range(2):
        first, count = part * Z // 2, Z // 2
        for z in range(first, first + count):
            here = slice(z * own, (z + 1) * own)
            scores = score_ref[here, :]
            weight_ref[here, :] = (
                0.5 * jnp.exp(scores - row_lse[here])
                + 0.5 * jnp.exp(scores - col_lse)
                - jnp.where(targets[:own, z:z + 1] - base == ids, 1.0, 0.0)
            )
        here = pl.ds(first * own, count * own)
        stores.append(pltpu.make_async_copy(weight_ref.at[here], weight_out.at[here], out_sems.at[0, part]))
        stores[-1].start()
        high, low = split(weight_ref[first * own:(first + count) * own, :])
        total = None
        for left, right in ((high, col_high), (high, col_low), (low, col_high)):
            term = jnp.dot(left, right, preferred_element_type=jnp.float32)
            total = term if total is None else total + term
        here = pl.ds(first, count)
        grad_ref[here] = (scale_ref[0] * total).reshape(count, own, total.shape[1])
        stores.append(pltpu.make_async_copy(grad_ref.at[here], grad_out.at[here], out_sems.at[1, part]))
        stores[-1].start()
    for store in stores:
        store.wait()


def local(row_embed, col_embed, logit_scale, targets):
    own, width = row_embed.shape
    plane, across, along, core = (lax.axis_index(a) for a in ALL)
    scale = logit_scale.reshape(1)
    cols = to_all(col_embed, ("x", "y", "core"), PLANE).reshape(PLANE * own, width)
    rows = lax.all_gather(row_embed, "z", axis=0, tiled=True)
    row_count, col_count = rows.shape[0], cols.shape[0]

    numbers = jnp.pad(targets.astype(jnp.float32), (0, LANES - own)).reshape(1, LANES)
    scores, col_message, row_message = pl.pallas_call(
        score_kernel,
        out_shape=(
            jax.ShapeDtypeStruct((row_count, col_count), jnp.float32),
            pltpu.HBM((PLANE, 8, LANES), jnp.float32),
            pltpu.HBM((Z, 8, LANES), jnp.float32),
        ),
        in_specs=[SMEM, VMEM, VMEM, VMEM],
        out_specs=(ANY, HBM, HBM),
        scratch_shapes=[
            pltpu.VMEM((row_count, col_count), jnp.float32),
            pltpu.VMEM((PLANE, 8, LANES), jnp.float32),
            pltpu.VMEM((Z, 8, LANES), jnp.float32),
            pltpu.SemaphoreType.DMA((3,)),
        ],
        compiler_params=PARAMS,
        name="scores",
    )(scale, rows, cols, numbers)

    heard_col = lax.all_to_all(col_message, ("x", "y", "core"), 0, 0, tiled=True)
    heard_col, row_message = lax.optimization_barrier((heard_col, row_message))
    heard_row = lax.all_to_all(row_message, "z", 0, 0, tiled=True)

    weights, grad_rows = pl.pallas_call(
        weight_kernel,
        out_shape=(
            pltpu.HBM((row_count, col_count), jnp.float32),
            pltpu.HBM((Z, own, width), jnp.float32),
        ),
        in_specs=[SMEM, SMEM, VMEM, ANY, ANY, ANY],
        out_specs=(HBM, HBM),
        scratch_shapes=[
            pltpu.VMEM((row_count, col_count), jnp.float32),
            pltpu.VMEM((PLANE, 8, LANES), jnp.float32),
            pltpu.VMEM((Z, 8, LANES), jnp.float32),
            pltpu.VMEM((row_count, col_count), jnp.float32),
            pltpu.VMEM((Z, own, width), jnp.float32),
            pltpu.SemaphoreType.DMA((3,)),
            pltpu.SemaphoreType.DMA((2, 2)),
        ],
        compiler_params=PARAMS,
        name="weights",
    )(scale, (plane * col_count).astype(jnp.float32).reshape(1), cols, scores, heard_col, heard_row)
    row_parts = lax.all_to_all(grad_rows, "z", 0, 0, tiled=True)
    grad_cols = lax.dot_general(
        weights, rows, (((0,), (0,)), ((), ())),
        precision=lax.Precision.HIGH, preferred_element_type=jnp.float32,
    ).reshape(SIDE, SIDE, CORE, own, width)
    col_sum = home(grad_cols, "core", CORE, 2, core)
    col_sum = home(col_sum, "y", SIDE, 1, along)
    col_sum = home(col_sum, "x", SIDE, 0, across)
    return jnp.sum(row_parts, axis=0), logit_scale * col_sum


def solution(mesh):
    grid = Mesh(mesh.devices.reshape(Z, SIDE, SIDE, CORE), ALL)
    placed = P(ALL, None)
    return jax.shard_map(
        local, mesh=grid, in_specs=(placed, placed, P(), P(ALL)), out_specs=(placed, placed), check_vma=False
    )
```

```python
import jax
import jax.numpy as jnp
from jax import lax
from jax.experimental import pallas as pl
from jax.experimental.pallas import tpu as pltpu
from jax.sharding import Mesh, PartitionSpec as P

ALL = ("z", "x", "y", "core")
Z, SIDE, CORE = 16, 4, 2
PLANE = SIDE * SIDE * CORE
LANES = 128
SMEM = pl.BlockSpec(memory_space=pltpu.SMEM)
VMEM = pl.BlockSpec(memory_space=pltpu.VMEM)
ANY = pl.BlockSpec(memory_space=pl.ANY)
HBM = pl.BlockSpec(memory_space=pltpu.HBM)
PARAMS = pltpu.CompilerParams(vmem_limit_bytes=48 * 1024 * 1024)


def repeat_kernel(block_ref, out, sems):
    copies = [pltpu.make_async_copy(block_ref, out.at[k], sems.at[k]) for k in range(out.shape[0])]
    for copy in copies:
        copy.start()
    for copy in copies:
        copy.wait()


def to_all(block, axes, count):
    sent = pl.pallas_call(
        repeat_kernel,
        out_shape=pltpu.HBM((count,) + block.shape, block.dtype),
        in_specs=[VMEM],
        out_specs=HBM,
        scratch_shapes=[pltpu.SemaphoreType.DMA((count,))],
        name="repeat",
    )(block)
    return lax.all_to_all(sent, axes, 0, 0, tiled=True)


def shift(block, axis, count, by):
    return lax.ppermute(block, axis, [(i, (i + by) % count) for i in range(count)])


def home(parts, axis, count, dim, me):
    def part(by):
        return lax.dynamic_index_in_dim(parts, (me - by + count) % count, dim, keepdims=False)

    total = part(0)
    for by in range(1, count):
        total = total + shift(part(by), axis, count, -by)
    return total


def score_kernel(
    scale_ref, row_ref, col_ref, target_ref, score_out, col_out, row_out, score_ref, col_part, row_part, sems
):
    stores = [
        pltpu.make_async_copy(source, target, sems.at[k])
        for k, (source, target) in enumerate(((score_ref, score_out), (row_part, row_out), (col_part, col_out)))
    ]
    scores = scale_ref[0] * lax.dot_general(
        row_ref[...], col_ref[...], (((1,), (1,)), ((), ())),
        precision=lax.Precision.HIGHEST, preferred_element_type=jnp.float32,
    )
    score_ref[...] = scores
    stores[0].start()
    used = scores.shape[0] // LANES
    for k in range(used):
        part = scores[k * LANES:(k + 1) * LANES]
        top = jnp.max(part, axis=1, keepdims=True)
        lse = top + jnp.log(jnp.sum(jnp.exp(part - top), axis=1, keepdims=True))
        lse = jnp.transpose(jnp.broadcast_to(lse, (LANES, LANES)))[:1]
        row_part[:, k, :] = jnp.broadcast_to(lse, (row_part.shape[0], LANES))
    row_part[:, used, :] = jnp.broadcast_to(target_ref[...], (row_part.shape[0], LANES))
    row_part[:, used + 1:, :] = jnp.zeros_like(row_part[:, used + 1:, :])
    stores[1].start()
    top = jnp.max(scores, axis=0, keepdims=True)
    lse = top + jnp.log(jnp.sum(jnp.exp(scores - top), axis=0, keepdims=True))
    used = lse.shape[1] // LANES
    for k in range(used):
        col_part[:, k, :] = jnp.broadcast_to(lse[:, k * LANES:(k + 1) * LANES], (col_part.shape[0], LANES))
    col_part[:, used:, :] = jnp.zeros_like(col_part[:, used:, :])
    stores[2].start()
    for store in stores:
        store.wait()


def split(values):
    high = values.astype(jnp.bfloat16)
    return high, (values - high.astype(jnp.float32)).astype(jnp.bfloat16)


def combined(heard):
    top = jnp.max(heard, axis=0)
    return top + jnp.log(jnp.sum(jnp.exp(heard - top[None]), axis=0))


def weight_kernel(
    scale_ref, base_ref, col_ref, score_in, heard_col_in, heard_row_in,
    weight_out, grad_out, score_ref, heard_col_ref, heard_row_ref, weight_ref, grad_ref, sems, out_sems,
):
    fetches = [
        pltpu.make_async_copy(source, target, sems.at[k])
        for k, (source, target) in enumerate(
            ((heard_row_in, heard_row_ref), (heard_col_in, heard_col_ref), (score_in, score_ref))
        )
    ]
    for fetch in fetches:
        fetch.start()
    row_count, col_count = score_ref.shape
    own = grad_ref.shape[1]
    col_high, col_low = split(col_ref[...])
    place = lax.broadcasted_iota(jnp.int32, (own, col_count), 1)
    half = col_count // CORE
    place_core = (place >= half).astype(jnp.int32)
    place = place - place_core * half
    chip = jnp.zeros_like(place)
    for k in range(1, PLANE // CORE):
        chip = chip + (place >= k * own).astype(jnp.int32)
    ids = (place + (chip + place_core) * own).astype(jnp.float32)
    base = base_ref[0]
    for fetch in fetches:
        fetch.wait()
    col_lse = combined(heard_col_ref[...])
    col_lse = jnp.concatenate([col_lse[k:k + 1] for k in range(col_count // LANES)], axis=1)
    row_lse = combined(heard_row_ref[...])
    row_lse = jnp.concatenate(
        [jnp.transpose(jnp.broadcast_to(row_lse[k:k + 1], (LANES, LANES))) for k in range(row_count // LANES)], axis=0
    )[:, :1]
    targets = jnp.transpose(
        jnp.concatenate([heard_row_ref[:, row_count // LANES, :], jnp.zeros((LANES - Z, LANES), jnp.float32)], axis=0)
    )
    stores = []
    for part in range(2):
        first, count = part * Z // 2, Z // 2
        for z in range(first, first + count):
            here = slice(z * own, (z + 1) * own)
            scores = score_ref[here, :]
            weight_ref[here, :] = (
                0.5 * jnp.exp(scores - row_lse[here])
                + 0.5 * jnp.exp(scores - col_lse)
                - jnp.where(targets[:own, z:z + 1] - base == ids, 1.0, 0.0)
            )
        here = pl.ds(first * own, count * own)
        stores.append(pltpu.make_async_copy(weight_ref.at[here], weight_out.at[here], out_sems.at[0, part]))
        stores[-1].start()
        high, low = split(weight_ref[first * own:(first + count) * own, :])
        total = None
        for left, right in ((high, col_high), (high, col_low), (low, col_high)):
            term = jnp.dot(left, right, preferred_element_type=jnp.float32)
            total = term if total is None else total + term
        here = pl.ds(first, count)
        grad_ref[here] = (scale_ref[0] * total).reshape(count, own, total.shape[1])
        stores.append(pltpu.make_async_copy(grad_ref.at[here], grad_out.at[here], out_sems.at[1, part]))
        stores[-1].start()
    for store in stores:
        store.wait()


def local(row_embed, col_embed, logit_scale, targets):
    own, width = row_embed.shape
    plane, across, along, core = (lax.axis_index(a) for a in ALL)
    scale = logit_scale.reshape(1)
    cols = to_all(col_embed, ("core", "x", "y"), PLANE).reshape(PLANE * own, width)
    rows = lax.all_gather(row_embed, "z", axis=0, tiled=True)
    row_count, col_count = rows.shape[0], cols.shape[0]

    numbers = jnp.pad(targets.astype(jnp.float32), (0, LANES - own)).reshape(1, LANES)
    scores, col_message, row_message = pl.pallas_call(
        score_kernel,
        out_shape=(
            jax.ShapeDtypeStruct((row_count, col_count), jnp.float32),
            pltpu.HBM((PLANE, 8, LANES), jnp.float32),
            pltpu.HBM((Z, 8, LANES), jnp.float32),
        ),
        in_specs=[SMEM, VMEM, VMEM, VMEM],
        out_specs=(ANY, HBM, HBM),
        scratch_shapes=[
            pltpu.VMEM((row_count, col_count), jnp.float32),
            pltpu.VMEM((PLANE, 8, LANES), jnp.float32),
            pltpu.VMEM((Z, 8, LANES), jnp.float32),
            pltpu.SemaphoreType.DMA((3,)),
        ],
        compiler_params=PARAMS,
        name="scores",
    )(scale, rows, cols, numbers)

    heard_col = lax.all_to_all(col_message, ("core", "x", "y"), 0, 0, tiled=True)
    heard_col, row_message = lax.optimization_barrier((heard_col, row_message))
    heard_row = lax.all_to_all(row_message, "z", 0, 0, tiled=True)
    heard_col = pltpu.with_memory_space_constraint(heard_col, pltpu.HBM)

    weights, grad_rows = pl.pallas_call(
        weight_kernel,
        out_shape=(
            pltpu.HBM((row_count, col_count), jnp.float32),
            pltpu.HBM((Z, own, width), jnp.float32),
        ),
        in_specs=[SMEM, SMEM, VMEM, ANY, ANY, ANY],
        out_specs=(HBM, HBM),
        scratch_shapes=[
            pltpu.VMEM((row_count, col_count), jnp.float32),
            pltpu.VMEM((PLANE, 8, LANES), jnp.float32),
            pltpu.VMEM((Z, 8, LANES), jnp.float32),
            pltpu.VMEM((row_count, col_count), jnp.float32),
            pltpu.VMEM((Z, own, width), jnp.float32),
            pltpu.SemaphoreType.DMA((3,)),
            pltpu.SemaphoreType.DMA((2, 2)),
        ],
        compiler_params=PARAMS,
        name="weights",
    )(scale, (plane * col_count).astype(jnp.float32).reshape(1), cols, scores, heard_col, heard_row)
    row_parts = lax.all_to_all(grad_rows, "z", 0, 0, tiled=True)

    def grad_cols(of_core):
        half = col_count // CORE
        return lax.dot_general(
            lax.dynamic_slice(weights, (0, of_core * half), (row_count, half)), rows, (((0,), (0,)), ((), ())),
            precision=lax.Precision.HIGH, preferred_element_type=jnp.float32,
        ).reshape(SIDE, SIDE, own, width)

    given = shift(grad_cols(1 - core), "core", CORE, 1)
    col_sum = home(grad_cols(core) + given, "y", SIDE, 1, along)
    col_sum = home(col_sum, "x", SIDE, 0, across)
    return jnp.sum(row_parts, axis=0), logit_scale * col_sum


def solution(mesh):
    grid = Mesh(mesh.devices.reshape(Z, SIDE, SIDE, CORE), ALL)
    placed = P(ALL, None)
    return jax.shard_map(
        local, mesh=grid, in_specs=(placed, placed, P(), P(ALL)), out_specs=(placed, placed), check_vma=False
    )
```

```python
import jax
import jax.numpy as jnp
from jax import lax
from jax.experimental import pallas as pl
from jax.experimental.pallas import tpu as pltpu
from jax.sharding import Mesh, PartitionSpec as P

ALL = ("z", "x", "y", "core")
Z, SIDE, CORE = 16, 4, 2
PLANE = SIDE * SIDE * CORE
LANES = 128
SMEM = pl.BlockSpec(memory_space=pltpu.SMEM)
VMEM = pl.BlockSpec(memory_space=pltpu.VMEM)
ANY = pl.BlockSpec(memory_space=pl.ANY)
HBM = pl.BlockSpec(memory_space=pltpu.HBM)
PARAMS = pltpu.CompilerParams(vmem_limit_bytes=48 * 1024 * 1024)


def repeat_kernel(block_ref, out, sems):
    copies = [pltpu.make_async_copy(block_ref, out.at[k], sems.at[k]) for k in range(out.shape[0])]
    for copy in copies:
        copy.start()
    for copy in copies:
        copy.wait()


def to_all(block, axes, count):
    sent = pl.pallas_call(
        repeat_kernel,
        out_shape=pltpu.HBM((count,) + block.shape, block.dtype),
        in_specs=[VMEM],
        out_specs=HBM,
        scratch_shapes=[pltpu.SemaphoreType.DMA((count,))],
        name="repeat",
    )(block)
    return lax.all_to_all(sent, axes, 0, 0, tiled=True)


def shift(block, axis, count, by):
    return lax.ppermute(block, axis, [(i, (i + by) % count) for i in range(count)])


def home(parts, axis, count, dim, me):
    def part(by):
        return lax.dynamic_index_in_dim(parts, (me - by + count) % count, dim, keepdims=False)

    total = part(0)
    for by in range(1, count):
        total = total + shift(part(by), axis, count, -by)
    return total


def score_kernel(
    scale_ref, row_ref, col_ref, target_ref, score_out, col_out, row_out, score_ref, col_part, row_part, sems
):
    stores = [
        pltpu.make_async_copy(source, target, sems.at[k])
        for k, (source, target) in enumerate(((score_ref, score_out), (row_part, row_out), (col_part, col_out)))
    ]
    scores = scale_ref[0] * lax.dot_general(
        row_ref[...], col_ref[...], (((1,), (1,)), ((), ())),
        precision=lax.Precision.HIGHEST, preferred_element_type=jnp.float32,
    )
    score_ref[...] = scores
    stores[0].start()
    used = scores.shape[0] // LANES
    for k in range(used):
        part = scores[k * LANES:(k + 1) * LANES]
        top = jnp.max(part, axis=1, keepdims=True)
        lse = top + jnp.log(jnp.sum(jnp.exp(part - top), axis=1, keepdims=True))
        lse = jnp.transpose(jnp.broadcast_to(lse, (LANES, LANES)))[:1]
        row_part[:, k, :] = jnp.broadcast_to(lse, (row_part.shape[0], LANES))
    row_part[:, used, :] = jnp.broadcast_to(target_ref[...], (row_part.shape[0], LANES))
    stores[1].start()
    top = jnp.max(scores, axis=0, keepdims=True)
    lse = top + jnp.log(jnp.sum(jnp.exp(scores - top), axis=0, keepdims=True))
    used = lse.shape[1] // LANES
    for k in range(used):
        col_part[:, k, :] = jnp.broadcast_to(lse[:, k * LANES:(k + 1) * LANES], (col_part.shape[0], LANES))
    col_part[:, used:, :] = jnp.zeros_like(col_part[:, used:, :])
    stores[2].start()
    for store in stores:
        store.wait()


def split(values):
    high = values.astype(jnp.bfloat16)
    return high, (values - high.astype(jnp.float32)).astype(jnp.bfloat16)


def combined(heard):
    top = jnp.max(heard, axis=0)
    return top + jnp.log(jnp.sum(jnp.exp(heard - top[None]), axis=0))


def weight_kernel(
    scale_ref, base_ref, col_ref, score_ref, heard_col_in, heard_row_in,
    weight_out, grad_out, heard_col_ref, heard_row_ref, weight_ref, grad_ref, sems, out_sems,
):
    fetches = [
        pltpu.make_async_copy(source, target, sems.at[k])
        for k, (source, target) in enumerate(
            ((heard_row_in, heard_row_ref), (heard_col_in, heard_col_ref))
        )
    ]
    for fetch in fetches:
        fetch.start()
    row_count, col_count = score_ref.shape
    own = grad_ref.shape[1]
    col_high, col_low = split(col_ref[...])
    place = lax.broadcasted_iota(jnp.int32, (own, col_count), 1)
    half = col_count // CORE
    place_core = (place >= half).astype(jnp.int32)
    place = place - place_core * half
    chip = jnp.zeros_like(place)
    for k in range(1, PLANE // CORE):
        chip = chip + (place >= k * own).astype(jnp.int32)
    ids = (place + (chip + place_core) * own).astype(jnp.float32)
    base = base_ref[0]
    for fetch in fetches:
        fetch.wait()
    col_lse = combined(heard_col_ref[...])
    col_lse = jnp.concatenate([col_lse[k:k + 1] for k in range(col_count // LANES)], axis=1)
    row_lse = combined(heard_row_ref[...])
    row_lse = jnp.concatenate(
        [jnp.transpose(jnp.broadcast_to(row_lse[k:k + 1], (LANES, LANES))) for k in range(row_count // LANES)], axis=0
    )[:, :1]
    targets = jnp.transpose(
        jnp.concatenate([heard_row_ref[:, row_count // LANES, :], jnp.zeros((LANES - Z, LANES), jnp.float32)], axis=0)
    )
    stores = []
    for part in range(2):
        first, count = part * Z // 2, Z // 2
        for z in range(first, first + count):
            here = slice(z * own, (z + 1) * own)
            scores = score_ref[here, :]
            weight_ref[here, :] = (
                0.5 * jnp.exp(scores - row_lse[here])
                + 0.5 * jnp.exp(scores - col_lse)
                - jnp.where(targets[:own, z:z + 1] - base == ids, 1.0, 0.0)
            )
        here = pl.ds(first * own, count * own)
        stores.append(pltpu.make_async_copy(weight_ref.at[here], weight_out.at[here], out_sems.at[0, part]))
        stores[-1].start()
        high, low = split(weight_ref[first * own:(first + count) * own, :])
        total = None
        for left, right in ((high, col_high), (high, col_low), (low, col_high)):
            term = jnp.dot(left, right, preferred_element_type=jnp.float32)
            total = term if total is None else total + term
        here = pl.ds(first, count)
        grad_ref[here] = (scale_ref[0] * total).reshape(count, own, total.shape[1])
        stores.append(pltpu.make_async_copy(grad_ref.at[here], grad_out.at[here], out_sems.at[1, part]))
        stores[-1].start()
    for store in stores:
        store.wait()


def local(row_embed, col_embed, logit_scale, targets):
    own, width = row_embed.shape
    plane, across, along, core = (lax.axis_index(a) for a in ALL)
    scale = logit_scale.reshape(1)
    cols = to_all(col_embed, ("core", "x", "y"), PLANE).reshape(PLANE * own, width)
    rows = lax.all_gather(row_embed, "z", axis=0, tiled=True)
    row_count, col_count = rows.shape[0], cols.shape[0]

    numbers = jnp.pad(targets.astype(jnp.float32), (0, LANES - own)).reshape(1, LANES)
    scores, col_message, row_message = pl.pallas_call(
        score_kernel,
        out_shape=(
            jax.ShapeDtypeStruct((row_count, col_count), jnp.float32),
            pltpu.HBM((PLANE, 8, LANES), jnp.float32),
            pltpu.HBM((Z, 4, LANES), jnp.float32),
        ),
        in_specs=[SMEM, VMEM, VMEM, VMEM],
        out_specs=(ANY, HBM, HBM),
        scratch_shapes=[
            pltpu.VMEM((row_count, col_count), jnp.float32),
            pltpu.VMEM((PLANE, 8, LANES), jnp.float32),
            pltpu.VMEM((Z, 4, LANES), jnp.float32),
            pltpu.SemaphoreType.DMA((3,)),
        ],
        compiler_params=PARAMS,
        name="scores",
    )(scale, rows, cols, numbers)

    heard_col = lax.all_to_all(col_message, ("core", "x", "y"), 0, 0, tiled=True)
    heard_col, row_message = lax.optimization_barrier((heard_col, row_message))
    heard_row = lax.all_to_all(row_message, "z", 0, 0, tiled=True)
    heard_col = pltpu.with_memory_space_constraint(heard_col, pltpu.HBM)

    weights, grad_rows = pl.pallas_call(
        weight_kernel,
        out_shape=(
            pltpu.HBM((row_count, col_count), jnp.float32),
            pltpu.HBM((Z, own, width), jnp.float32),
        ),
        in_specs=[SMEM, SMEM, VMEM, VMEM, ANY, ANY],
        out_specs=(HBM, HBM),
        scratch_shapes=[
            pltpu.VMEM((PLANE, 8, LANES), jnp.float32),
            pltpu.VMEM((Z, 4, LANES), jnp.float32),
            pltpu.VMEM((row_count, col_count), jnp.float32),
            pltpu.VMEM((Z, own, width), jnp.float32),
            pltpu.SemaphoreType.DMA((2,)),
            pltpu.SemaphoreType.DMA((2, 2)),
        ],
        compiler_params=PARAMS,
        name="weights",
    )(scale, (plane * col_count).astype(jnp.float32).reshape(1), cols, scores, heard_col, heard_row)
    row_parts = lax.all_to_all(grad_rows, "z", 0, 0, tiled=True)

    def grad_cols(of_core):
        half = col_count // CORE
        return lax.dot_general(
            lax.dynamic_slice(weights, (0, of_core * half), (row_count, half)), rows, (((0,), (0,)), ((), ())),
            precision=lax.Precision.HIGH, preferred_element_type=jnp.float32,
        ).reshape(SIDE, SIDE, own, width)

    given = shift(grad_cols(1 - core), "core", CORE, 1)
    col_sum = home(grad_cols(core) + given, "y", SIDE, 1, along)
    col_sum = home(col_sum, "x", SIDE, 0, across)
    return jnp.sum(row_parts, axis=0), logit_scale * col_sum


def solution(mesh):
    grid = Mesh(mesh.devices.reshape(Z, SIDE, SIDE, CORE), ALL)
    placed = P(ALL, None)
    return jax.shard_map(
        local, mesh=grid, in_specs=(placed, placed, P(), P(ALL)), out_specs=(placed, placed), check_vma=False
    )
```

```python
import jax
import jax.numpy as jnp
from jax import lax
from jax.experimental import pallas as pl
from jax.experimental.pallas import tpu as pltpu
from jax.sharding import Mesh, PartitionSpec as P

ALL = ("z", "x", "y", "core")
Z, SIDE, CORE = 16, 4, 2
PLANE = SIDE * SIDE * CORE
LANES = 128
SMEM = pl.BlockSpec(memory_space=pltpu.SMEM)
VMEM = pl.BlockSpec(memory_space=pltpu.VMEM)
ANY = pl.BlockSpec(memory_space=pl.ANY)
HBM = pl.BlockSpec(memory_space=pltpu.HBM)
PARAMS = pltpu.CompilerParams(vmem_limit_bytes=48 * 1024 * 1024)


def repeat_kernel(block_ref, out, sems):
    copies = [pltpu.make_async_copy(block_ref, out.at[k], sems.at[k]) for k in range(out.shape[0])]
    for copy in copies:
        copy.start()
    for copy in copies:
        copy.wait()


def to_all(block, axes, count):
    sent = pl.pallas_call(
        repeat_kernel,
        out_shape=pltpu.HBM((count,) + block.shape, block.dtype),
        in_specs=[VMEM],
        out_specs=HBM,
        scratch_shapes=[pltpu.SemaphoreType.DMA((count,))],
        name="repeat",
    )(block)
    return lax.all_to_all(sent, axes, 0, 0, tiled=True)


def shift(block, axis, count, by):
    return lax.ppermute(block, axis, [(i, (i + by) % count) for i in range(count)])


def home(parts, axis, count, dim, me):
    def part(by):
        return lax.dynamic_index_in_dim(parts, (me - by + count) % count, dim, keepdims=False)

    total = part(0)
    for by in range(1, count):
        total = total + shift(part(by), axis, count, -by)
    return total


def score_kernel(
    scale_ref, row_ref, col_ref, target_ref, score_out, col_out, row_out, score_ref, col_part, row_part, sems
):
    stores = [
        pltpu.make_async_copy(source, target, sems.at[k])
        for k, (source, target) in enumerate(((score_ref, score_out), (row_part, row_out), (col_part, col_out)))
    ]
    scores = scale_ref[0] * lax.dot_general(
        row_ref[...], col_ref[...], (((1,), (1,)), ((), ())),
        precision=lax.Precision.HIGHEST, preferred_element_type=jnp.float32,
    )
    score_ref[...] = scores
    stores[0].start()
    used = scores.shape[0] // LANES
    for k in range(used):
        part = scores[k * LANES:(k + 1) * LANES]
        top = jnp.max(part, axis=1, keepdims=True)
        lse = top + jnp.log(jnp.sum(jnp.exp(part - top), axis=1, keepdims=True))
        lse = jnp.transpose(jnp.broadcast_to(lse, (LANES, LANES)))[:1]
        row_part[:, k, :] = jnp.broadcast_to(lse, (row_part.shape[0], LANES))
    row_part[:, used, :] = jnp.broadcast_to(target_ref[...], (row_part.shape[0], LANES))
    stores[1].start()
    top = jnp.max(scores, axis=0, keepdims=True)
    lse = top + jnp.log(jnp.sum(jnp.exp(scores - top), axis=0, keepdims=True))
    used = lse.shape[1] // LANES
    for k in range(used):
        col_part[:, k, :] = jnp.broadcast_to(lse[:, k * LANES:(k + 1) * LANES], (col_part.shape[0], LANES))
    col_part[:, used:, :] = jnp.zeros_like(col_part[:, used:, :])
    stores[2].start()
    for store in stores:
        store.wait()


def split(values):
    high = values.astype(jnp.bfloat16)
    return high, (values - high.astype(jnp.float32)).astype(jnp.bfloat16)


def combined(heard):
    top = jnp.max(heard, axis=0)
    return top + jnp.log(jnp.sum(jnp.exp(heard - top[None]), axis=0))


def fetched(pairs, sems):
    copies = [pltpu.make_async_copy(source, target, sems.at[k]) for k, (source, target) in enumerate(pairs)]
    for copy in copies:
        copy.start()
    for copy in copies:
        copy.wait()


def row_facts(heard_row_ref, row_count):
    row_lse = combined(heard_row_ref[...])
    row_lse = jnp.concatenate(
        [jnp.transpose(jnp.broadcast_to(row_lse[k:k + 1], (LANES, LANES))) for k in range(row_count // LANES)], axis=0
    )[:, :1]
    targets = jnp.transpose(
        jnp.concatenate([heard_row_ref[:, row_count // LANES, :], jnp.zeros((LANES - Z, LANES), jnp.float32)], axis=0)
    )
    return row_lse, targets


def column_ids(own, of_core):
    place = lax.broadcasted_iota(jnp.int32, (own, PLANE // CORE * own), 1)
    chip = jnp.zeros_like(place)
    for k in range(1, PLANE // CORE):
        chip = chip + (place >= k * own).astype(jnp.int32)
    return (place + (chip + of_core) * own).astype(jnp.float32)


def weigh(scores, row_lse, col_lse, targets, ids):
    return (
        0.5 * jnp.exp(scores - row_lse)
        + 0.5 * jnp.exp(scores - col_lse)
        - jnp.where(targets == ids, 1.0, 0.0)
    )


def row_kernel(
    scale_ref, base_ref, col_ref, score_ref, heard_col_in, heard_row_in,
    grad_out, heard_col_ref, heard_row_ref, weight_ref, grad_ref, sems, out_sems,
):
    row_count, col_count = score_ref.shape
    own = grad_ref.shape[1]
    fetched(((heard_row_in, heard_row_ref), (heard_col_in, heard_col_ref)), sems)
    col_high, col_low = split(col_ref[...])
    ids = jnp.concatenate([column_ids(own, c) for c in range(CORE)], axis=1)
    col_lse = combined(heard_col_ref[...])
    col_lse = jnp.concatenate([col_lse[k:k + 1] for k in range(col_count // LANES)], axis=1)
    row_lse, targets = row_facts(heard_row_ref, row_count)
    base = base_ref[0]
    stores = []
    for part in range(2):
        first, count = part * Z // 2, Z // 2
        for z in range(first, first + count):
            here = slice(z * own, (z + 1) * own)
            weight_ref[here, :] = weigh(score_ref[here, :], row_lse[here], col_lse, targets[:own, z:z + 1] - base, ids)
        high, low = split(weight_ref[first * own:(first + count) * own, :])
        total = None
        for left, right in ((high, col_high), (high, col_low), (low, col_high)):
            term = jnp.dot(left, right, preferred_element_type=jnp.float32)
            total = term if total is None else total + term
        here = pl.ds(first, count)
        grad_ref[here] = (scale_ref[0] * total).reshape(count, own, total.shape[1])
        stores.append(pltpu.make_async_copy(grad_ref.at[here], grad_out.at[here], out_sems.at[part]))
        stores[-1].start()
    for store in stores:
        store.wait()


def col_kernel(
    scale_ref, base_ref, core_ref, row_ref, score_ref, heard_col_in, heard_row_in,
    grad_out, heard_col_ref, heard_row_ref, lse_ref, weight_ref, grad_ref, sems,
):
    row_count, half = weight_ref.shape
    own = grad_ref.shape[1]
    fetched(((heard_row_in, heard_row_ref), (heard_col_in, heard_col_ref)), sems)
    of_core = core_ref[0]
    row_high, row_low = split(row_ref[...])
    ids = column_ids(own, of_core)
    lse_ref[...] = combined(heard_col_ref[...])
    used = half // LANES
    col_lse = jnp.concatenate([lse_ref[pl.ds(of_core * used + k, 1), :] for k in range(used)], axis=1)
    row_lse, targets = row_facts(heard_row_ref, row_count)
    base = base_ref[0]
    there = pl.ds(pl.multiple_of(of_core * half, LANES), half)
    for z in range(Z):
        here = slice(z * own, (z + 1) * own)
        weight_ref[here, :] = weigh(score_ref[here, there], row_lse[here], col_lse, targets[:own, z:z + 1] - base, ids)
    high, low = split(weight_ref[...])
    total = None
    for left, right in ((high, row_high), (high, row_low), (low, row_high)):
        term = lax.dot_general(left, right, (((0,), (0,)), ((), ())), preferred_element_type=jnp.float32)
        total = term if total is None else total + term
    grad_ref[...] = (scale_ref[0] * total).reshape(grad_ref.shape)
    store = pltpu.make_async_copy(grad_ref, grad_out, sems.at[2])
    store.start()
    store.wait()


def local(row_embed, col_embed, logit_scale, targets):
    own, width = row_embed.shape
    plane, across, along, core = (lax.axis_index(a) for a in ALL)
    scale = logit_scale.reshape(1)
    cols = to_all(col_embed, ("core", "x", "y"), PLANE).reshape(PLANE * own, width)
    rows = lax.all_gather(row_embed, "z", axis=0, tiled=True)
    row_count, col_count = rows.shape[0], cols.shape[0]

    numbers = jnp.pad(targets.astype(jnp.float32), (0, LANES - own)).reshape(1, LANES)
    scores, col_message, row_message = pl.pallas_call(
        score_kernel,
        out_shape=(
            jax.ShapeDtypeStruct((row_count, col_count), jnp.float32),
            pltpu.HBM((PLANE, 8, LANES), jnp.float32),
            pltpu.HBM((Z, 4, LANES), jnp.float32),
        ),
        in_specs=[SMEM, VMEM, VMEM, VMEM],
        out_specs=(ANY, HBM, HBM),
        scratch_shapes=[
            pltpu.VMEM((row_count, col_count), jnp.float32),
            pltpu.VMEM((PLANE, 8, LANES), jnp.float32),
            pltpu.VMEM((Z, 4, LANES), jnp.float32),
            pltpu.SemaphoreType.DMA((3,)),
        ],
        compiler_params=PARAMS,
        name="scores",
    )(scale, rows, cols, numbers)

    heard_col = lax.all_to_all(col_message, ("core", "x", "y"), 0, 0, tiled=True)
    heard_col, row_message = lax.optimization_barrier((heard_col, row_message))
    heard_row = lax.all_to_all(row_message, "z", 0, 0, tiled=True)
    heard_col = pltpu.with_memory_space_constraint(heard_col, pltpu.HBM)

    base = (plane * col_count).astype(jnp.float32).reshape(1)
    heard_scratch = [pltpu.VMEM((PLANE, 8, LANES), jnp.float32), pltpu.VMEM((Z, 4, LANES), jnp.float32)]
    grad_rows = pl.pallas_call(
        row_kernel,
        out_shape=pltpu.HBM((Z, own, width), jnp.float32),
        in_specs=[SMEM, SMEM, VMEM, VMEM, ANY, ANY],
        out_specs=HBM,
        scratch_shapes=heard_scratch + [
            pltpu.VMEM((row_count, col_count), jnp.float32),
            pltpu.VMEM((Z, own, width), jnp.float32),
            pltpu.SemaphoreType.DMA((2,)),
            pltpu.SemaphoreType.DMA((2,)),
        ],
        compiler_params=PARAMS,
        name="row_grads",
    )(scale, base, cols, scores, heard_col, heard_row)
    row_parts = lax.all_to_all(grad_rows, "z", 0, 0, tiled=True)

    def grad_cols(of_core):
        half = col_count // CORE
        return pl.pallas_call(
            col_kernel,
            out_shape=jax.ShapeDtypeStruct((SIDE * SIDE, own, width), jnp.float32),
            in_specs=[SMEM, SMEM, SMEM, VMEM, VMEM, ANY, ANY],
            out_specs=ANY,
            scratch_shapes=heard_scratch + [
                pltpu.VMEM((8, LANES), jnp.float32),
                pltpu.VMEM((row_count, half), jnp.float32),
                pltpu.VMEM((SIDE * SIDE, own, width), jnp.float32),
                pltpu.SemaphoreType.DMA((3,)),
            ],
            compiler_params=PARAMS,
            name="col_grads",
        )(scale, base, of_core.reshape(1), rows, scores, heard_col, heard_row).reshape(SIDE, SIDE, own, width)

    given = shift(grad_cols(1 - core), "core", CORE, 1)
    col_sum = home(grad_cols(core) + given, "y", SIDE, 1, along)
    col_sum = home(col_sum, "x", SIDE, 0, across)
    return jnp.sum(row_parts, axis=0), col_sum


def solution(mesh):
    grid = Mesh(mesh.devices.reshape(Z, SIDE, SIDE, CORE), ALL)
    placed = P(ALL, None)
    return jax.shard_map(
        local, mesh=grid, in_specs=(placed, placed, P(), P(ALL)), out_specs=(placed, placed), check_vma=False
    )
```

```python
import jax
import jax.numpy as jnp
from jax import lax
from jax.experimental import pallas as pl
from jax.experimental.pallas import tpu as pltpu
from jax.sharding import Mesh, PartitionSpec as P

ALL = ("z", "x", "y", "core")
Z, SIDE, CORE = 16, 4, 2
PLANE = SIDE * SIDE * CORE
LANES = 128
SMEM = pl.BlockSpec(memory_space=pltpu.SMEM)
VMEM = pl.BlockSpec(memory_space=pltpu.VMEM)
ANY = pl.BlockSpec(memory_space=pl.ANY)
HBM = pl.BlockSpec(memory_space=pltpu.HBM)
PARAMS = pltpu.CompilerParams(vmem_limit_bytes=48 * 1024 * 1024)


def repeat_kernel(block_ref, out, sems):
    copies = [pltpu.make_async_copy(block_ref, out.at[k], sems.at[k]) for k in range(out.shape[0])]
    for copy in copies:
        copy.start()
    for copy in copies:
        copy.wait()


def to_all(block, axes, count):
    sent = pl.pallas_call(
        repeat_kernel,
        out_shape=pltpu.HBM((count,) + block.shape, block.dtype),
        in_specs=[VMEM],
        out_specs=HBM,
        scratch_shapes=[pltpu.SemaphoreType.DMA((count,))],
        name="repeat",
    )(block)
    return lax.all_to_all(sent, axes, 0, 0, tiled=True)


def shift(block, axis, count, by):
    return lax.ppermute(block, axis, [(i, (i + by) % count) for i in range(count)])


def home(parts, axis, count, dim, me):
    def part(by):
        return lax.dynamic_index_in_dim(parts, (me - by + count) % count, dim, keepdims=False)

    total = part(0)
    for by in range(1, count):
        total = total + shift(part(by), axis, count, -by)
    return total


def score_kernel(scale_ref, row_ref, col_ref, score_out, col_out, score_ref, col_part, sems):
    stores = [
        pltpu.make_async_copy(source, target, sems.at[k])
        for k, (source, target) in enumerate(((score_ref, score_out), (col_part, col_out)))
    ]
    scores = scale_ref[0] * lax.dot_general(
        row_ref[...], col_ref[...], (((1,), (1,)), ((), ())),
        precision=lax.Precision.HIGHEST, preferred_element_type=jnp.float32,
    )
    score_ref[...] = scores
    stores[0].start()
    top = jnp.max(scores, axis=0, keepdims=True)
    lse = top + jnp.log(jnp.sum(jnp.exp(scores - top), axis=0, keepdims=True))
    used = lse.shape[1] // LANES
    for k in range(used):
        col_part[:, k, :] = jnp.broadcast_to(lse[:, k * LANES:(k + 1) * LANES], (col_part.shape[0], LANES))
    col_part[:, used:, :] = jnp.zeros_like(col_part[:, used:, :])
    stores[1].start()
    for store in stores:
        store.wait()


def row_message_kernel(score_ref, target_ref, row_out, row_part, sem):
    used = score_ref.shape[0] // LANES
    for k in range(used):
        part = score_ref[k * LANES:(k + 1) * LANES, :]
        top = jnp.max(part, axis=1, keepdims=True)
        lse = top + jnp.log(jnp.sum(jnp.exp(part - top), axis=1, keepdims=True))
        lse = jnp.transpose(jnp.broadcast_to(lse, (LANES, LANES)))[:1]
        row_part[:, k, :] = jnp.broadcast_to(lse, (row_part.shape[0], LANES))
    row_part[:, used, :] = jnp.broadcast_to(target_ref[...], (row_part.shape[0], LANES))
    store = pltpu.make_async_copy(row_part, row_out, sem)
    store.start()
    store.wait()


def split(values):
    high = values.astype(jnp.bfloat16)
    return high, (values - high.astype(jnp.float32)).astype(jnp.bfloat16)


def combined(heard):
    top = jnp.max(heard, axis=0)
    return top + jnp.log(jnp.sum(jnp.exp(heard - top[None]), axis=0))


def weight_kernel(
    scale_ref, base_ref, col_ref, score_ref, heard_col_in, heard_row_in,
    weight_out, grad_out, heard_col_ref, heard_row_ref, weight_ref, grad_ref, sems, out_sems,
):
    fetches = [
        pltpu.make_async_copy(source, target, sems.at[k])
        for k, (source, target) in enumerate(
            ((heard_row_in, heard_row_ref), (heard_col_in, heard_col_ref))
        )
    ]
    for fetch in fetches:
        fetch.start()
    row_count, col_count = score_ref.shape
    own = grad_ref.shape[1]
    col_high, col_low = split(col_ref[...])
    place = lax.broadcasted_iota(jnp.int32, (own, col_count), 1)
    half = col_count // CORE
    place_core = (place >= half).astype(jnp.int32)
    place = place - place_core * half
    chip = jnp.zeros_like(place)
    for k in range(1, PLANE // CORE):
        chip = chip + (place >= k * own).astype(jnp.int32)
    ids = (place + (chip + place_core) * own).astype(jnp.float32)
    base = base_ref[0]
    for fetch in fetches:
        fetch.wait()
    col_lse = combined(heard_col_ref[...])
    col_lse = jnp.concatenate([col_lse[k:k + 1] for k in range(col_count // LANES)], axis=1)
    row_lse = combined(heard_row_ref[...])
    row_lse = jnp.concatenate(
        [jnp.transpose(jnp.broadcast_to(row_lse[k:k + 1], (LANES, LANES))) for k in range(row_count // LANES)], axis=0
    )[:, :1]
    targets = jnp.transpose(
        jnp.concatenate([heard_row_ref[:, row_count // LANES, :], jnp.zeros((LANES - Z, LANES), jnp.float32)], axis=0)
    )
    stores = []
    for part in range(2):
        first, count = part * Z // 2, Z // 2
        for z in range(first, first + count):
            here = slice(z * own, (z + 1) * own)
            scores = score_ref[here, :]
            weight_ref[here, :] = (
                0.5 * jnp.exp(scores - row_lse[here])
                + 0.5 * jnp.exp(scores - col_lse)
                - jnp.where(targets[:own, z:z + 1] - base == ids, 1.0, 0.0)
            )
        here = pl.ds(first * own, count * own)
        stores.append(pltpu.make_async_copy(weight_ref.at[here], weight_out.at[here], out_sems.at[0, part]))
        stores[-1].start()
        high, low = split(weight_ref[first * own:(first + count) * own, :])
        total = None
        for left, right in ((high, col_high), (high, col_low), (low, col_high)):
            term = jnp.dot(left, right, preferred_element_type=jnp.float32)
            total = term if total is None else total + term
        here = pl.ds(first, count)
        grad_ref[here] = (scale_ref[0] * total).reshape(count, own, total.shape[1])
        stores.append(pltpu.make_async_copy(grad_ref.at[here], grad_out.at[here], out_sems.at[1, part]))
        stores[-1].start()
    for store in stores:
        store.wait()


def local(row_embed, col_embed, logit_scale, targets):
    own, width = row_embed.shape
    plane, across, along, core = (lax.axis_index(a) for a in ALL)
    scale = logit_scale.reshape(1)
    cols = to_all(col_embed, ("core", "x", "y"), PLANE).reshape(PLANE * own, width)
    rows = lax.all_gather(row_embed, "z", axis=0, tiled=True)
    row_count, col_count = rows.shape[0], cols.shape[0]

    numbers = jnp.pad(targets.astype(jnp.float32), (0, LANES - own)).reshape(1, LANES)
    scores, col_message = pl.pallas_call(
        score_kernel,
        out_shape=(
            jax.ShapeDtypeStruct((row_count, col_count), jnp.float32),
            pltpu.HBM((PLANE, 8, LANES), jnp.float32),
        ),
        in_specs=[SMEM, VMEM, VMEM],
        out_specs=(ANY, HBM),
        scratch_shapes=[
            pltpu.VMEM((row_count, col_count), jnp.float32),
            pltpu.VMEM((PLANE, 8, LANES), jnp.float32),
            pltpu.SemaphoreType.DMA((2,)),
        ],
        compiler_params=PARAMS,
        name="scores",
    )(scale, rows, cols)
    heard_col = lax.all_to_all(col_message, ("core", "x", "y"), 0, 0, tiled=True)
    row_message = pl.pallas_call(
        row_message_kernel,
        out_shape=pltpu.HBM((Z, 4, LANES), jnp.float32),
        in_specs=[VMEM, VMEM],
        out_specs=HBM,
        scratch_shapes=[pltpu.VMEM((Z, 4, LANES), jnp.float32), pltpu.SemaphoreType.DMA],
        compiler_params=PARAMS,
        cost_estimate=pl.CostEstimate(flops=4 * row_count * col_count, bytes_accessed=4 * row_count * col_count, transcendentals=row_count * col_count),
        name="row_message",
    )(scores, numbers)
    heard_col, row_message = lax.optimization_barrier((heard_col, row_message))
    heard_row = lax.all_to_all(row_message, "z", 0, 0, tiled=True)
    heard_col = pltpu.with_memory_space_constraint(heard_col, pltpu.HBM)

    weights, grad_rows = pl.pallas_call(
        weight_kernel,
        out_shape=(
            pltpu.HBM((row_count, col_count), jnp.float32),
            pltpu.HBM((Z, own, width), jnp.float32),
        ),
        in_specs=[SMEM, SMEM, VMEM, VMEM, ANY, ANY],
        out_specs=(HBM, HBM),
        scratch_shapes=[
            pltpu.VMEM((PLANE, 8, LANES), jnp.float32),
            pltpu.VMEM((Z, 4, LANES), jnp.float32),
            pltpu.VMEM((row_count, col_count), jnp.float32),
            pltpu.VMEM((Z, own, width), jnp.float32),
            pltpu.SemaphoreType.DMA((2,)),
            pltpu.SemaphoreType.DMA((2, 2)),
        ],
        compiler_params=PARAMS,
        name="weights",
    )(scale, (plane * col_count).astype(jnp.float32).reshape(1), cols, scores, heard_col, heard_row)
    row_parts = lax.all_to_all(grad_rows, "z", 0, 0, tiled=True)

    def grad_cols(of_core):
        half = col_count // CORE
        return lax.dot_general(
            lax.dynamic_slice(weights, (0, of_core * half), (row_count, half)), rows, (((0,), (0,)), ((), ())),
            precision=lax.Precision.HIGH, preferred_element_type=jnp.float32,
        ).reshape(SIDE, SIDE, own, width)

    given = shift(grad_cols(1 - core), "core", CORE, 1)
    col_sum = home(grad_cols(core) + given, "y", SIDE, 1, along)
    col_sum = home(col_sum, "x", SIDE, 0, across)
    return jnp.sum(row_parts, axis=0), logit_scale * col_sum


def solution(mesh):
    grid = Mesh(mesh.devices.reshape(Z, SIDE, SIDE, CORE), ALL)
    placed = P(ALL, None)
    return jax.shard_map(
        local, mesh=grid, in_specs=(placed, placed, P(), P(ALL)), out_specs=(placed, placed), check_vma=False
    )
```

```python
import jax
import jax.numpy as jnp
from jax import lax
from jax.experimental import pallas as pl
from jax.experimental.pallas import tpu as pltpu
from jax.sharding import Mesh, PartitionSpec as P

ALL = ("z", "x", "y", "core")
Z, SIDE, CORE = 16, 4, 2
PLANE = SIDE * SIDE * CORE
LANES = 128
SMEM = pl.BlockSpec(memory_space=pltpu.SMEM)
VMEM = pl.BlockSpec(memory_space=pltpu.VMEM)
ANY = pl.BlockSpec(memory_space=pl.ANY)
HBM = pl.BlockSpec(memory_space=pltpu.HBM)
PARAMS = pltpu.CompilerParams(vmem_limit_bytes=48 * 1024 * 1024)


def repeat_kernel(block_ref, out, sems):
    copies = [pltpu.make_async_copy(block_ref, out.at[k], sems.at[k]) for k in range(out.shape[0])]
    for copy in copies:
        copy.start()
    for copy in copies:
        copy.wait()


def to_all(block, axes, count):
    sent = pl.pallas_call(
        repeat_kernel,
        out_shape=pltpu.HBM((count,) + block.shape, block.dtype),
        in_specs=[VMEM],
        out_specs=HBM,
        scratch_shapes=[pltpu.SemaphoreType.DMA((count,))],
        name="repeat",
    )(block)
    return lax.all_to_all(sent, axes, 0, 0, tiled=True)


def shift(block, axis, count, by):
    return lax.ppermute(block, axis, [(i, (i + by) % count) for i in range(count)])


def home(parts, axis, count, dim, me):
    def part(by):
        return lax.dynamic_index_in_dim(parts, (me - by + count) % count, dim, keepdims=False)

    total = part(0)
    for by in range(1, count):
        total = total + shift(part(by), axis, count, -by)
    return total


def score_kernel(scale_ref, row_ref, col_ref, score_out, col_out, score_ref, col_part, sems):
    stores = [
        pltpu.make_async_copy(source, target, sems.at[k])
        for k, (source, target) in enumerate(((score_ref, score_out), (col_part, col_out)))
    ]
    scores = scale_ref[0] * lax.dot_general(
        row_ref[...], col_ref[...], (((1,), (1,)), ((), ())),
        precision=lax.Precision.HIGHEST, preferred_element_type=jnp.float32,
    )
    score_ref[...] = scores
    stores[0].start()
    top = jnp.max(scores, axis=0, keepdims=True)
    lse = top + jnp.log(jnp.sum(jnp.exp(scores - top), axis=0, keepdims=True))
    used = lse.shape[1] // LANES
    for k in range(used):
        col_part[:, k, :] = jnp.broadcast_to(lse[:, k * LANES:(k + 1) * LANES], (col_part.shape[0], LANES))
    col_part[:, used:, :] = jnp.zeros_like(col_part[:, used:, :])
    stores[1].start()
    for store in stores:
        store.wait()


def row_message_kernel(score_ref, target_ref, row_out, row_part, sem):
    used = score_ref.shape[0] // LANES
    for k in range(used):
        part = score_ref[k * LANES:(k + 1) * LANES, :]
        top = jnp.max(part, axis=1, keepdims=True)
        lse = top + jnp.log(jnp.sum(jnp.exp(part - top), axis=1, keepdims=True))
        lse = jnp.transpose(jnp.broadcast_to(lse, (LANES, LANES)))[:1]
        row_part[:, k, :] = jnp.broadcast_to(lse, (row_part.shape[0], LANES))
    row_part[:, used, :] = jnp.broadcast_to(target_ref[...], (row_part.shape[0], LANES))
    store = pltpu.make_async_copy(row_part, row_out, sem)
    store.start()
    store.wait()


def split(values):
    high = values.astype(jnp.bfloat16)
    return high, (values - high.astype(jnp.float32)).astype(jnp.bfloat16)


def combined(heard):
    top = jnp.max(heard, axis=0)
    return top + jnp.log(jnp.sum(jnp.exp(heard - top[None]), axis=0))


def weight_kernel(
    scale_ref, base_ref, col_ref, score_ref, heard_col_in, heard_row_in,
    weight_out, grad_out, heard_col_ref, heard_row_ref, weight_ref, grad_ref, sems, out_sems,
):
    fetches = [
        pltpu.make_async_copy(source, target, sems.at[k])
        for k, (source, target) in enumerate(
            ((heard_row_in, heard_row_ref), (heard_col_in, heard_col_ref))
        )
    ]
    for fetch in fetches:
        fetch.start()
    row_count, col_count = score_ref.shape
    own = grad_ref.shape[1]
    col_high, col_low = split(col_ref[...])
    place = lax.broadcasted_iota(jnp.int32, (own, col_count), 1)
    half = col_count // CORE
    place_core = (place >= half).astype(jnp.int32)
    place = place - place_core * half
    chip = jnp.zeros_like(place)
    for k in range(1, PLANE // CORE):
        chip = chip + (place >= k * own).astype(jnp.int32)
    ids = (place + (chip + place_core) * own).astype(jnp.float32)
    base = base_ref[0]
    for fetch in fetches:
        fetch.wait()
    col_lse = combined(heard_col_ref[...])
    col_lse = jnp.concatenate([col_lse[k:k + 1] for k in range(col_count // LANES)], axis=1)
    row_lse = combined(heard_row_ref[...])
    row_lse = jnp.concatenate(
        [jnp.transpose(jnp.broadcast_to(row_lse[k:k + 1], (LANES, LANES))) for k in range(row_count // LANES)], axis=0
    )[:, :1]
    targets = jnp.transpose(
        jnp.concatenate([heard_row_ref[:, row_count // LANES, :], jnp.zeros((LANES - Z, LANES), jnp.float32)], axis=0)
    )
    for z in range(Z):
        here = slice(z * own, (z + 1) * own)
        weight_ref[here, :] = (
            0.5 * jnp.exp(score_ref[here, :] - row_lse[here])
            + 0.5 * jnp.exp(score_ref[here, :] - col_lse)
            - jnp.where(targets[:own, z:z + 1] - base == ids, 1.0, 0.0)
        )
    stores = []
    high, low = split(weight_ref[...])
    half = grad_ref.shape[2] // 2
    for part in range(2):
        here = slice(part * half, (part + 1) * half)
        total = None
        for left, right in ((high, col_high), (high, col_low), (low, col_high)):
            term = jnp.dot(left, right[:, here], preferred_element_type=jnp.float32)
            total = term if total is None else total + term
        grad_ref[:, :, here] = (scale_ref[0] * total).reshape(grad_ref.shape[0], own, half)
        there = pl.ds(part * half, half)
        stores.append(pltpu.make_async_copy(grad_ref.at[:, :, there], grad_out.at[:, :, there], out_sems.at[part]))
        stores[-1].start()
        if part == 0:
            stores.append(pltpu.make_async_copy(weight_ref, weight_out, out_sems.at[2]))
            stores[-1].start()
    for store in stores:
        store.wait()


def local(row_embed, col_embed, logit_scale, targets):
    own, width = row_embed.shape
    plane, across, along, core = (lax.axis_index(a) for a in ALL)
    scale = logit_scale.reshape(1)
    cols = to_all(col_embed, ("core", "x", "y"), PLANE).reshape(PLANE * own, width)
    rows = lax.all_gather(row_embed, "z", axis=0, tiled=True)
    row_count, col_count = rows.shape[0], cols.shape[0]

    numbers = jnp.pad(targets.astype(jnp.float32), (0, LANES - own)).reshape(1, LANES)
    scores, col_message = pl.pallas_call(
        score_kernel,
        out_shape=(
            jax.ShapeDtypeStruct((row_count, col_count), jnp.float32),
            pltpu.HBM((PLANE, 8, LANES), jnp.float32),
        ),
        in_specs=[SMEM, VMEM, VMEM],
        out_specs=(ANY, HBM),
        scratch_shapes=[
            pltpu.VMEM((row_count, col_count), jnp.float32),
            pltpu.VMEM((PLANE, 8, LANES), jnp.float32),
            pltpu.SemaphoreType.DMA((2,)),
        ],
        compiler_params=PARAMS,
        name="scores",
    )(scale, rows, cols)
    heard_col = lax.all_to_all(col_message, ("core", "x", "y"), 0, 0, tiled=True)
    row_message = pl.pallas_call(
        row_message_kernel,
        out_shape=pltpu.HBM((Z, 4, LANES), jnp.float32),
        in_specs=[VMEM, VMEM],
        out_specs=HBM,
        scratch_shapes=[pltpu.VMEM((Z, 4, LANES), jnp.float32), pltpu.SemaphoreType.DMA],
        compiler_params=PARAMS,
        cost_estimate=pl.CostEstimate(flops=4 * row_count * col_count, bytes_accessed=4 * row_count * col_count, transcendentals=row_count * col_count),
        name="row_message",
    )(scores, numbers)
    heard_col, row_message = lax.optimization_barrier((heard_col, row_message))
    heard_row = lax.all_to_all(row_message, "z", 0, 0, tiled=True)
    heard_col = pltpu.with_memory_space_constraint(heard_col, pltpu.HBM)

    weights, grad_rows = pl.pallas_call(
        weight_kernel,
        out_shape=(
            pltpu.HBM((row_count, col_count), jnp.float32),
            pltpu.HBM((Z, own, width), jnp.float32),
        ),
        in_specs=[SMEM, SMEM, VMEM, VMEM, ANY, ANY],
        out_specs=(HBM, HBM),
        scratch_shapes=[
            pltpu.VMEM((PLANE, 8, LANES), jnp.float32),
            pltpu.VMEM((Z, 4, LANES), jnp.float32),
            pltpu.VMEM((row_count, col_count), jnp.float32),
            pltpu.VMEM((Z, own, width), jnp.float32),
            pltpu.SemaphoreType.DMA((2,)),
            pltpu.SemaphoreType.DMA((3,)),
        ],
        compiler_params=PARAMS,
        name="weights",
    )(scale, (plane * col_count).astype(jnp.float32).reshape(1), cols, scores, heard_col, heard_row)
    row_parts = lax.all_to_all(grad_rows, "z", 0, 0, tiled=True)

    def grad_cols(of_core):
        half = col_count // CORE
        return lax.dot_general(
            lax.dynamic_slice(weights, (0, of_core * half), (row_count, half)), rows, (((0,), (0,)), ((), ())),
            precision=lax.Precision.HIGH, preferred_element_type=jnp.float32,
        ).reshape(SIDE, SIDE, own, width)

    given = shift(grad_cols(1 - core), "core", CORE, 1)
    col_sum = home(grad_cols(core) + given, "y", SIDE, 1, along)
    col_sum = home(col_sum, "x", SIDE, 0, across)
    return jnp.sum(row_parts, axis=0), logit_scale * col_sum


def solution(mesh):
    grid = Mesh(mesh.devices.reshape(Z, SIDE, SIDE, CORE), ALL)
    placed = P(ALL, None)
    return jax.shard_map(
        local, mesh=grid, in_specs=(placed, placed, P(), P(ALL)), out_specs=(placed, placed), check_vma=False
    )
```
